128 devices in a mesh: req: 16 (over z_hi, y, core), head: 8 (over x, z_lo).
Axes of the slice: x: 4, y: 4, z: 4 (z_hi: 2, z_lo: 2; z = z_hi * 2 + z_lo), core: 2. Of those that a mesh axis runs over, the one named last changes fastest.
Arguments:
- tokens: bfloat16 [24576, 16384], P('req', 'head'), may hold values from -2000 to 2000
- norm_gain: bfloat16 [16384], P('head'), may hold values from 0.099609375 to 1.8984375
- kv_weight: bfloat16 [16384, 2048], P('head'), may hold values from -0.0234375 to 0.0234375
- prompt_lens: int32 [16, 32], P('req'), may hold values from 1 to 64, 1536 in all within a row
- owner_of: int32 [512, 1], P('req'), may hold values from 0 to 15; in each aligned block of 32 rows (0 to 31, 32 to 63, ...) at most 4 rows name the same one
- arr_query: bfloat16 [4, 512, 16384], P(None, 'req', 'head'), may hold values from -128 to 128
- arr_step_kv: bfloat16 [4, 512, 2048], P(None, 'req', 'head'), may hold values from -3 to 3
- prefix_kv: bfloat16 [16384, 2048], P('req', 'head'), may hold values from -6 to 6
- res_query: bfloat16 [4, 512, 16384], P(None, 'req', 'head'), may hold values from -128 to 128
- res_cache: bfloat16 [512, 512, 2048], P('req', None, 'head'), may hold values from -6 to 6
- res_step_kv: bfloat16 [4, 512, 2048], P(None, 'req', 'head'), may hold values from -3 to 3
- cache_lens: int32 [512], P('req'), may hold values from 2 to 512
Outputs:
- arr_out: float32 [4, 512, 16384], P(None, 'req', 'head')
- res_out: float32 [4, 512, 16384], P(None, 'req', 'head')
The draws below stay inside these ranges and needn't reach their ends.
Inputs may be any that keep to these rules, and one draw needn't show every extreme that they name: `owner_of`: among the 32 requests of one index of req no owner appears more than 4 times.
All inputs are finite; a program needn't handle non-finite values.
Results may differ from the reference program's by a relative error of at most 0.012.
Values may be sent and summed in bfloat16 or wider, within the bound.
A program may use at most 128 MiB of HBM per device.

```python
import math
import jax
import jax.numpy as jnp
import numpy as np
from jax import lax

D = 16384
HD = 128
GROUP = 16
KVH = 8
QH = 128
STEPS = 4
MAXLEN = 64
PREFIX = 1024
CACHE = 512
RES_DEV = 32
TOK_DEV = 1536
NPD = 32
CAP = 4
TOKENS = 24576
PREQS = 512
RES_TOTAL = 512
N_REQ = 16
N_HEAD = 8


def value_factor():
    return jnp.where(jnp.arange(2 * HD) < HD, 1.0, 0.5).astype(jnp.float32)


def drawn_keys(key, request_rows, row_count):
    key = jax.random.fold_in(key, 32)
    return jnp.clip(jax.random.normal(key, (request_rows, row_count, KVH, 2 * HD), jnp.float32), -6.0, 6.0) * value_factor()


def draw_tokens(key, part):
    key = jax.random.fold_in(key, 23)
    first_key, second_key, third_key = jax.random.split(key, 3)
    rising = jnp.exp(jax.random.uniform(second_key, (1, D), jnp.float32, 0.0, math.log(10.0))) * 3.0 ** (jnp.arange(D, dtype=jnp.float32) / D)
    row_scale = jnp.exp(jax.random.uniform(first_key, (TOKENS, 1), jnp.float32, 0.0, math.log(10.0)))
    drawn = jnp.clip(jax.random.normal(third_key, (TOKENS, D), jnp.float32), -6.0, 6.0)
    return (drawn * row_scale * rising).astype(jnp.bfloat16)


def draw_prefix_kv(key, part):
    owners = RES_TOTAL // RES_DEV
    drawn = drawn_keys(key, owners, PREFIX)
    return drawn.reshape(owners * PREFIX, KVH * 2 * HD).astype(jnp.bfloat16)


def draw_res_cache(key, part):
    key = jax.random.fold_in(key, 0)
    drawn = drawn_keys(key, RES_TOTAL, CACHE)
    return drawn.reshape(RES_TOTAL, CACHE, KVH * 2 * HD).astype(jnp.bfloat16)


def draw_arr_query(key, part):
    key = jax.random.fold_in(key, 22)
    drawn = jnp.clip(jax.random.normal(key, (STEPS, PREQS, KVH * GROUP * HD), jnp.float32), -6.0, 6.0)
    return drawn.astype(jnp.bfloat16)


def draw_res_query(key, part):
    key = jax.random.fold_in(key, 0)
    key = jax.random.fold_in(key, 25)
    drawn = jnp.clip(jax.random.normal(key, (STEPS, RES_TOTAL, KVH * GROUP * HD), jnp.float32), -6.0, 6.0)
    return drawn.astype(jnp.bfloat16)


def draw_cache_lens(key, part):
    key = jax.random.fold_in(key, 24)
    first_key, second_key, third_key = jax.random.split(key, 3)
    blocks = RES_TOTAL // RES_DEV
    ceiling = jax.random.randint(first_key, (blocks, 1), max(CACHE // 8, 3), CACHE + 1)
    lengths = jax.random.randint(second_key, (blocks, RES_DEV), 2, ceiling + 1)
    forced = jax.random.randint(third_key, (blocks, 1), 0, RES_DEV)
    lengths = jnp.where(jnp.arange(RES_DEV)[None, :] == forced, CACHE, lengths)
    return lengths.reshape(RES_TOTAL).astype(jnp.int32)


def block_scale(rng, shape, cuts, low, largest):
    def one(position, parts):
        heights = jax.random.uniform(jax.random.fold_in(jax.random.fold_in(rng, 6), position), (parts,), jnp.float32, low / len(cuts), largest / len(cuts))
        return jnp.repeat(jnp.exp(heights), shape[position] // parts).reshape((-1,) + (1,) * (len(shape) - position - 1))

    level = one(*cuts[0])
    for cut in cuts[1:]:
        level = level * one(*cut)
    return level


def profile(amount, total, limit, slope):
    weights = [(1 << 20) // math.isqrt(rank ** slope) + 1 for rank in range(2, amount + 1)]
    spare, given = total - limit - (amount - 1), [1] * (amount - 1)
    while spare > 0:
        free = [i for i in range(amount - 1) if given[i] < limit]
        whole, budget = sum([weights[i] for i in free]), spare
        for i in free:
            extra = min(limit - given[i], max(1, budget * weights[i] // whole), spare)
            given[i] = given[i] + extra
            spare = spare - extra
    return np.array([limit] + given)


def uneven(stream_key, amount, total, most, skew):
    if amount == 2:
        one = jax.random.randint(stream_key, (), max(1, total - most), min(most, total - 1) + 1)
        return jnp.stack([one, total - one])
    tallies = jnp.asarray(profile(amount, total, most, skew), jnp.int32)
    couples = (amount - 1) // 2
    source_of, sink = tallies[1:1 + 2 * couples:2], tallies[2:2 + 2 * couples:2]
    slack = jnp.minimum(source_of - 1, most - sink)
    moved = jax.random.randint(jax.random.fold_in(stream_key, 1), (couples,), 0, 1 << 20) % (slack + 1)
    tallies = tallies.at[1:1 + 2 * couples:2].set(source_of - moved).at[2:2 + 2 * couples:2].set(sink + moved)
    return tallies[jax.random.permutation(jax.random.fold_in(stream_key, 2), amount)]


def deal_out(own_key, own, number, rows, amount, top, most, lean):
    ranking = jax.random.permutation(own_key, amount)
    packed, common = load_shares(amount, rows * top, most, lean, True), load_shares(amount, rows * top, most, lean, False)
    places = jnp.arange(amount)

    def named(sizes, turn):
        used = int((sizes > 0).sum())
        fixed = max(1, used // 4)
        passed = fixed + (places - fixed + turn * (used - fixed)) % max(1, amount - fixed)
        return jnp.zeros((amount,), jnp.int32).at[ranking[jnp.where(places < fixed, places, passed)]].set(jnp.asarray(sizes, jnp.int32))

    sizes = jnp.where(number % 4 == 0, named(packed, number // 4), named(common, number - number // 4 - 1))
    mixed = jax.random.permutation(jax.random.fold_in(own, 3), amount)
    giver, receiver = mixed[0:amount // 2 * 2:2], mixed[1:amount // 2 * 2:2]
    margin = jnp.minimum(sizes[giver] - 1, most - sizes[receiver]) // 2
    margin = jnp.where((giver == ranking[0]) | (receiver == ranking[0]) | (sizes[receiver] == 0), 0, jnp.maximum(margin, 0))
    passed = jax.random.randint(jax.random.fold_in(own, 4), (amount // 2,), 0, 1 << 20) % (margin + 1)
    sizes = sizes.at[giver].add(-passed).at[receiver].add(passed)
    labels = jnp.searchsorted(jnp.cumsum(sizes), jnp.arange(rows * top), side="right").astype(jnp.int32)
    table = labels.reshape(top, rows).T
    table = table[jax.random.permutation(jax.random.fold_in(own, 1), rows)]
    turn = jax.random.randint(jax.random.fold_in(own, 2), (rows, 1), 0, top)
    return jnp.take_along_axis(table, (jnp.arange(top)[None, :] + turn) % top, axis=1)


def load_shares(amount, total, bound, slope, full):
    portions = [(1 << 20) // math.isqrt(rank ** slope) + 1 for rank in range(1, amount + 1)]
    largest = bound if full else min(bound, max(-(-total // amount), total * portions[0] // sum(portions)))
    least = 1 if total - largest >= amount - 1 else 0
    holding, rest = [largest] + [least] * (amount - 1), total - largest - least * (amount - 1)
    while rest > 0:
        free = [i for i in range(1, amount) if holding[i] < largest] or [i for i in range(1, amount) if holding[i] < bound]
        mass, remaining = sum([portions[i] for i in free]), rest
        for i in free:
            addition = min(bound - holding[i], max(1, remaining * portions[i] // mass), rest)
            holding[i] = holding[i] + addition
            rest = rest - addition
    return np.array(holding)


def gaussian(key, extent, scale, reach, cuts=(), held_as=jnp.bfloat16):
    values = scale * jax.random.normal(key, extent, jnp.float32)
    if cuts:
        values = values * block_scale(key, extent, cuts, -0.22, 0.18)
    return jnp.clip(values, -reach, reach).astype(held_as)


def setup_inputs(seed: int = 0) -> dict:
    key_of = jax.random.split(jax.random.key(seed), 13)
    tokens = draw_tokens(jax.random.fold_in(key_of[12], 71), 0)
    norm_gain = jnp.clip(1.0 + 0.18 * jax.random.normal(key_of[1], (D,), jnp.float32), 0.099609375, 1.8984375).astype(jnp.bfloat16)
    kv_weight = gaussian(key_of[2], (D, KVH * 2 * HD), (4 * D) ** -0.5, 0.0234375, ((0, 8),))
    prompt_lens = jax.vmap(lambda own: uneven(own, NPD, TOK_DEV, MAXLEN, 2))(jax.random.split(key_of[3], N_REQ)).reshape((N_REQ, NPD)).astype(jnp.int32)
    owner_of_keys = jax.random.split(jax.random.fold_in(key_of[4], 1), PREQS // NPD)
    owner_of_turns = jax.random.permutation(jax.random.fold_in(key_of[4], 3), PREQS // NPD)
    owner_of = jax.vmap(lambda own, number: deal_out(jax.random.fold_in(key_of[4], 2), own, number, NPD, N_REQ, 1, CAP, 2))(owner_of_keys, owner_of_turns).reshape((PREQS, 1))
    arr_query = draw_arr_query(jax.random.fold_in(key_of[12], 71), 0)
    arr_step_kv = gaussian(key_of[6], (STEPS, PREQS, KVH * 2 * HD), 0.5, 3.0, ((1, 16), (2, 8)))
    prefix_kv = draw_prefix_kv(jax.random.fold_in(key_of[12], 71), 0)
    res_query = draw_res_query(jax.random.fold_in(key_of[12], 71), 0)
    res_cache = draw_res_cache(jax.random.fold_in(key_of[12], 71), 0)
    res_step_kv = gaussian(key_of[10], (STEPS, RES_TOTAL, KVH * 2 * HD), 0.5, 3.0, ((1, 16), (2, 8)))
    cache_lens = draw_cache_lens(jax.random.fold_in(key_of[12], 71), 0)
    return {"tokens": tokens, "norm_gain": norm_gain, "kv_weight": kv_weight, "prompt_lens": prompt_lens, "owner_of": owner_of, "arr_query": arr_query, "arr_step_kv": arr_step_kv, "prefix_kv": prefix_kv, "res_query": res_query, "res_cache": res_cache, "res_step_kv": res_step_kv, "cache_lens": cache_lens}


norm_epsilon = 1e-05

def attend_reference(queries, key_rows, valid_mask):
    keys_only = key_rows[..., :HD].astype(jnp.float32)
    values = key_rows[..., HD:].astype(jnp.float32)
    scores = jnp.einsum('thgd,lhd->thgl', queries.astype(jnp.float32), keys_only) * HD ** (-0.5)
    scores = jnp.where(valid_mask[:, None, None, :], scores, -1e+30)
    highest = lax.optimization_barrier(jnp.max(scores, axis=-1, keepdims=True))
    raised = jnp.exp(scores - highest)
    weights = (raised / lax.optimization_barrier(jnp.sum(raised, axis=-1, keepdims=True))).astype(jnp.bfloat16)
    result = jnp.einsum('thgl,lhd->thgd', weights.astype(jnp.float32), values)
    return result.astype(jnp.float32)

def reference(tokens, norm_gain, kv_weight, prompt_lens, owner_of, arr_query, arr_step_kv, prefix_kv, res_query, res_cache, res_step_kv, cache_lens):
    kv_width = KVH * 2 * HD
    slice_width = D // N_HEAD
    weight_float = kv_weight.astype(jnp.float32).reshape(N_HEAD, slice_width, kv_width)
    gain_float = norm_gain.astype(jnp.float32)

    def project(token_block):
        as_float = token_block.astype(jnp.float32)
        inverse = lax.rsqrt(lax.optimization_barrier(jnp.mean(as_float * as_float, axis=1)) + norm_epsilon)
        scaled = (as_float * gain_float).astype(jnp.bfloat16)
        partials = jnp.einsum('bhd,hdk->hbk', scaled.astype(jnp.float32).reshape(-1, N_HEAD, slice_width), weight_float)
        partials = lax.optimization_barrier(partials.astype(jnp.bfloat16)).astype(jnp.float32)
        return (lax.optimization_barrier(jnp.sum(partials, axis=0)) * inverse[:, None]).astype(jnp.bfloat16)
    new_kv = lax.map(project, tokens.reshape(N_REQ, TOK_DEV, D)).reshape(TOKENS, kv_width)
    padded = jnp.concatenate([new_kv, jnp.zeros((MAXLEN, kv_width), new_kv.dtype)], axis=0)
    offsets = (jnp.cumsum(prompt_lens, axis=1) - prompt_lens + jnp.arange(N_REQ, dtype=jnp.int32)[:, None] * TOK_DEV).reshape(PREQS).astype(jnp.int32)
    flat_lens = prompt_lens.reshape(PREQS)
    prefixes = prefix_kv.reshape(N_REQ, PREFIX, KVH, 2 * HD)
    step_mask = jnp.arange(STEPS)[None, :] <= jnp.arange(STEPS)[:, None]
    positions = jnp.arange(MAXLEN)

    def one_arrival(request):
        row_start = offsets[request]
        shared = prefixes[owner_of[request, 0]]
        prompt = lax.dynamic_slice(padded, (row_start, jnp.zeros((), jnp.int32)), (MAXLEN, kv_width)).reshape(MAXLEN, KVH, 2 * HD)
        recent = lax.dynamic_index_in_dim(arr_step_kv, request, 1, keepdims=False).reshape(STEPS, KVH, 2 * HD)
        key_rows = jnp.concatenate([shared, prompt, recent], axis=0)
        prompt_mask = jnp.broadcast_to(positions[None, :] < flat_lens[request], (STEPS, MAXLEN))
        valid_mask = jnp.concatenate([jnp.ones((STEPS, PREFIX), jnp.bool_), prompt_mask, step_mask], axis=1)
        queries = lax.dynamic_index_in_dim(arr_query, request, 1, keepdims=False).reshape(STEPS, KVH, GROUP, HD)
        return attend_reference(queries, key_rows, valid_mask).reshape(STEPS, QH * HD)
    arr_out = jnp.transpose(lax.map(one_arrival, jnp.arange(PREQS, dtype=jnp.int32)), (1, 0, 2))
    cache_positions = jnp.arange(CACHE)

    def one_resident(request):
        cached = res_cache[request].reshape(CACHE, KVH, 2 * HD)
        recent = lax.dynamic_index_in_dim(res_step_kv, request, 1, keepdims=False).reshape(STEPS, KVH, 2 * HD)
        key_rows = jnp.concatenate([cached, recent], axis=0)
        cache_mask = jnp.broadcast_to(cache_positions[None, :] < cache_lens[request], (STEPS, CACHE))
        valid_mask = jnp.concatenate([cache_mask, step_mask], axis=1)
        queries = lax.dynamic_index_in_dim(res_query, request, 1, keepdims=False).reshape(STEPS, KVH, GROUP, HD)
        return attend_reference(queries, key_rows, valid_mask).reshape(STEPS, QH * HD)
    res_out = jnp.transpose(lax.map(one_resident, jnp.arange(RES_TOTAL, dtype=jnp.int32)), (1, 0, 2))
    return (arr_out, res_out)
```

```python
import functools
import math

import jax
import jax.numpy as jnp
from jax import lax
from jax.experimental import pallas as pl
from jax.experimental.pallas import tpu as pltpu
from jax.sharding import PartitionSpec as P

D = 16384
HD = 128
PAIR = 2 * HD
STEPS = 4
GROUP = 16
ROWS = STEPS * GROUP
TOK = 1536
WIDTH = 2048
NC = 6
RB = TOK // NC
NPD = 32
OWNERS = 16
CAP = 4
PREFIX = 1024
CACHE = 512
STEP_PAD = 16
WINDOW = 80
EPS = 1e-05
LOG2E = math.log2(math.e)
SCALE = HD**-0.5 * LOG2E
MESH = pl.DeviceIdType.MESH

ORDER = ((2, 1), (1, 1), (3, 1), (2, 0), (0, 1), (1, 0), (3, 0), (0, 0))
F32 = jnp.float32
BF16 = jnp.bfloat16
NT = (((1,), (1,)), ((), ()))
TN = (((0,), (0,)), ((), ()))


def mod(a, n):
    return lax.rem(a, n)


def kernel(
    tokens, gain, weight, lens, owner, arr_query, arr_step, prefix, res_query, cache, res_step, cache_lens,
    out_res, kv, pacc, plse, aq, astep, req_slot, req_start,
    rq, rstep, done_res,
    tok, w, cach, pre, s1, s2, p20, p01, pd, p00, s1r, s2r, r2r, z2r, xr,
    ssq, slot_query,
    tok_sem, w_sem, cache_sem,
    s1_ss, s1_rs, s2_ss, s2_rs, r2_ss, r2_rs, z2_ss, z2_rs, x_ss, x_rs,
    ssq_ss, ssq_rs, pre_ss, pre_rs,
):
    r = lax.axis_index("req")
    h = lax.axis_index("head")
    x, zl = h // 2, mod(h, 2)
    zh, y, core = r // 8, mod(r // 2, 4), mod(r, 2)

    def head_at(dx, zf):
        return mod(x + dx, 4) * 2 + mod(zl + zf, 2)

    def req_at(zx, dy, cx):
        return mod(zh + zx, 2) * 8 + mod(y + dy, 4) * 2 + mod(core + cx, 2)

    def tok_copy(c):
        return pltpu.make_async_copy(tokens.at[c], tok.at[c], tok_sem.at[c])

    def w_copy(k):
        cols = pl.ds(pl.multiple_of(head_at(*ORDER[k]) * PAIR, PAIR), PAIR)
        return pltpu.make_async_copy(weight.at[:, cols], w.at[k], w_sem.at[k])

    def cache_copy(g):
        return pltpu.make_async_copy(cache.at[g], cach.at[g], cache_sem.at[g])

    tok_copy(0).start()
    w_copy(0).start()

    barrier = pltpu.get_barrier_semaphore()
    peers = [(r, mod(h + k, 8)) for k in range(1, 8)]
    peers += [(req_at(1, 0, 0), h), (req_at(0, 1, 0), h), (req_at(0, 3, 0), h), (req_at(0, 0, 1), h)]
    for peer in peers:
        pl.semaphore_signal(barrier, inc=1, device_id=peer, device_id_type=MESH)
    pl.semaphore_wait(barrier, len(peers))

    def remote(src, dst, ss, rs, device):
        return pltpu.make_async_remote_copy(
            src_ref=src, dst_ref=dst, send_sem=ss, recv_sem=rs, device_id=device, device_id_type=MESH
        )

    turn = 1 + 2 * core
    where = {"own": 0, "back": 4 - turn, "front": turn, "far": 2}
    names = [(zx, name, cx) for zx in range(2) for name in where for cx in range(2)][1:]
    held = dict(zip(names, pre))
    held[0, "own", 0] = prefix
    sends = []

    def send_prefix(name, to_name, to):
        n = len(sends)
        cp = remote(held[name], held[to_name], pre_ss.at[n], pre_rs.at[names.index(to_name)], (req_at(*to), h))
        cp.start()
        sends.append(cp)

    def wait_prefix(name):
        n = names.index(name)
        remote(held[name], held[name], pre_ss.at[0], pre_rs.at[n], (req_at(0, 0, 1), h)).wait_recv()

    def own_prefix(zx):
        send_prefix((zx, "own", 0), (zx, "back", 0), (0, turn, 0))
        send_prefix((zx, "own", 0), (zx, "front", 0), (0, 4 - turn, 0))
        send_prefix((zx, "own", 0), (zx, "own", 1), (0, 0, 1))

    def near_prefix(zx):
        wait_prefix((zx, "back", 0))
        send_prefix((zx, "back", 0), (zx, "far", 0), (0, turn, 0))
        send_prefix((zx, "back", 0), (zx, "back", 1), (0, 0, 1))
        wait_prefix((zx, "front", 0))
        send_prefix((zx, "front", 0), (zx, "front", 1), (0, 0, 1))

    def far_prefix(zx):
        wait_prefix((zx, "far", 0))
        send_prefix((zx, "far", 0), (zx, "far", 1), (0, 0, 1))

    def partner_prefix():
        wait_prefix((1, "own", 0))
        own_prefix(1)

    send_prefix((0, "own", 0), (1, "own", 0), (1, 0, 0))
    own_prefix(0)
    for c in range(1, NC):
        tok_copy(c).start()
    for k in range(1, 8):
        w_copy(k).start()
    for g in range(8):
        cache_copy(g).start()

    z_dev = (r, head_at(0, 1))

    def x_dev(step):
        return (r, mod(x + step, 4) * 2 + zl)

    def s1_copy(c):
        return remote(s1.at[c], s1r.at[c], s1_ss.at[c], s1_rs.at[c], z_dev)

    def s2_copy(d, c):
        return remote(s2.at[d, c], s2r.at[d, c], s2_ss.at[d, c], s2_rs.at[d, c], x_dev(1 + 2 * d))

    def r2_copy(c):
        return remote(p20.at[c], r2r.at[c], r2_ss.at[c], r2_rs.at[c], x_dev(1 + 2 * mod(c, 2)))

    def z2_copy(c):
        return remote(p01.at[c], z2r.at[c], z2_ss.at[c], z2_rs.at[c], z_dev)

    def x_copy(d, c):
        return remote(pd.at[d, c], xr.at[d, c], x_ss.at[d, c], x_rs.at[d, c], x_dev(1 + 2 * d))

    def project(k, c):
        return jnp.dot(tok[c], w[k], preferred_element_type=F32).astype(BF16)

    for k in range(3):
        w_copy(k).wait()

    def first(c, carry):
        tok_copy(c).wait()
        acc = []
        for b in range(4):
            rows = slice(b * (RB // 4), (b + 1) * (RB // 4))
            total = None
            for j in range(WIDTH // HD):
                cols = slice(j * HD, (j + 1) * HD)
                part = tok[c, rows, cols].astype(F32)
                square = part * part
                total = square if total is None else total + square
                tok[c, rows, cols] = (part * gain[cols].astype(F32)[None, :]).astype(BF16)
            acc.append(total)
        total = jnp.concatenate(acc, axis=0)
        s1[c] = project(0, c)
        s1_copy(c).start()
        s2[0, c] = project(1, c)
        s2_copy(0, c).start()
        s2[1, c] = project(2, c)
        s2_copy(1, c).start()
        row = lax.dot_general(
            jnp.ones((8, HD), F32), total, NT, precision=lax.Precision.HIGHEST, preferred_element_type=F32
        )
        ssq[h, c] = row[0:1, :]
        return carry

    lax.fori_loop(0, NC, first, 0)

    def ssq_copy(k):
        return remote(ssq.at[h], ssq.at[h], ssq_ss.at[k], ssq_rs.at[k], (r, mod(h + k + 1, 8)))

    for k in range(7):
        ssq_copy(k).start()

    def by_request(n, carry):
        mine = owner[n]

        def look(m, found):
            before = (m < n).astype(jnp.int32)
            return found[0] + (owner[m] == mine).astype(jnp.int32) * before, found[1] + lens[m] * before

        rank, begin = lax.fori_loop(0, NPD, look, (jnp.int32(0), jnp.int32(0)))
        req_slot[n] = mine * CAP + rank
        req_start[n] = begin
        return carry

    def by_rows(natural, rows):
        for t in range(STEPS):
            for g in range(GROUP):
                rows[:, t * GROUP + g, :] = natural[t, :, g * HD:(g + 1) * HD].astype(rows.dtype)

    def queries_by_slot():
        lax.fori_loop(0, NPD, by_request, 0)
        request = lax.broadcasted_iota(jnp.int32, (OWNERS * CAP, NPD), 1)
        held = jnp.full((OWNERS * CAP, NPD), -1, jnp.int32)
        for n in range(NPD):
            held = jnp.where(request == n, req_slot[n], held)
        slot = lax.broadcasted_iota(jnp.int32, (OWNERS * CAP, NPD), 0)
        chosen = jnp.where(held == slot, 1.0, 0.0).astype(BF16)
        for t in range(STEPS):
            for g in range(GROUP):
                part = jnp.dot(chosen, arr_query[t, :, g * HD:(g + 1) * HD], preferred_element_type=F32)
                slot_query[:, t * GROUP + g, :] = part

    def steps_by_rows(natural, rows):
        rows[...] = jnp.zeros(rows.shape, rows.dtype)
        for t in range(STEPS):
            for half in range(2):
                rows[half, :, t, :] = natural[t, :, half * HD:(half + 1) * HD].astype(rows.dtype)

    by_rows(res_query, rq)
    steps_by_rows(res_step, rstep)
    by_rows(arr_query, aq)
    steps_by_rows(arr_step, astep)

    def add(*parts):
        return functools.reduce(jnp.add, [part.astype(F32) for part in parts])

    def straight(c, carry):
        pd[0, c] = project(5, c)
        pd[1, c] = project(6, c)
        x_copy(1 - mod(c, 2), c).start()
        return carry

    def second(c, carry):
        p20[c] = project(3, c)
        p01[c] = project(4, c)
        p00[c] = project(7, c)
        return carry

    def to_far(c):
        s1_copy(c).wait_recv()
        p20[c] = add(p20[c], s1r[c]).astype(BF16)
        r2_copy(c).start()

    def to_near(c):
        d = mod(c, 2)
        r2_copy(c).wait_recv()
        pd[d, c] = add(pd[d, c], r2r[c]).astype(BF16)
        x_copy(d, c).start()

    def to_z(c, carry):
        s2_copy(0, c).wait_recv()
        s2_copy(1, c).wait_recv()
        p01[c] = add(p01[c], s2r[0, c], s2r[1, c]).astype(BF16)
        z2_copy(c).start()
        return carry

    col = lax.broadcasted_iota(jnp.int32, (ROWS, CACHE + STEP_PAD), 1)
    row_step = lax.broadcasted_iota(jnp.int32, (ROWS, CACHE + STEP_PAD), 0) // GROUP
    recent_valid = (col >= CACHE) & (col - CACHE <= row_step)

    def residents(i, carry):
        group = [i * 4 + k for k in range(4)]
        keys, values = [
            [
                jnp.concatenate([cach[i, k, :, half * HD:(half + 1) * HD], rstep[half, n].astype(BF16)], axis=0)
                for k, n in enumerate(group)
            ]
            for half in range(2)
        ]
        scores = []
        for k, n in enumerate(group):
            part = lax.dot_general(rq[n].astype(BF16), keys[k], NT, preferred_element_type=F32)
            scores.append(jnp.where((col < cache_lens[n]) | recent_valid, part, -1e30))
        scores = jnp.concatenate(scores, axis=0)
        highest = jnp.max(scores, axis=1, keepdims=True)
        raised = jnp.exp2((scores - highest) * SCALE)
        total = jnp.sum(raised, axis=1, keepdims=True)
        raised = raised.astype(BF16)
        for k, n in enumerate(group):
            rows = slice(k * ROWS, (k + 1) * ROWS)
            result = jnp.dot(raised[rows], values[k], preferred_element_type=F32)
            done_res[n] = result / total[rows]
        return carry

    def shared(zx, name, cx):
        rows = held[zx, name, cx]
        dy = where[name] if cx == 0 else mod(4 - where[name], 4)
        slots = pl.ds(pl.multiple_of(req_at(zx, dy, cx) * CAP, CAP), CAP)
        queries = slot_query[slots].reshape(CAP * ROWS, HD).astype(BF16)
        scores = lax.dot_general(queries, rows[:, :HD], NT, preferred_element_type=F32)
        highest = jnp.max(scores, axis=1, keepdims=True)
        raised = jnp.exp2((scores - highest) * SCALE)
        total = jnp.sum(raised, axis=1, keepdims=True)
        result = jnp.dot(raised.astype(BF16), rows[:, HD:], preferred_element_type=F32) / total
        level = jnp.broadcast_to(highest * SCALE + jnp.log2(total), (CAP * ROWS, HD))
        pacc[slots] = result.astype(BF16).reshape(CAP, ROWS, HD)
        plse[slots] = level.reshape(CAP, ROWS, HD)

    def shared_pair(zx, name):
        shared(zx, name, 0)
        wait_prefix((zx, name, 1))
        shared(zx, name, 1)

    def middle(c, carry):
        to_far(c)
        to_near(c - 1)
        return residents(c, carry)

    w_copy(5).wait()
    w_copy(6).wait()
    lax.fori_loop(0, NC, straight, 0)
    w_copy(3).wait()
    w_copy(4).wait()
    w_copy(7).wait()
    lax.fori_loop(0, NC, second, 0)
    queries_by_slot()
    for g in range(8):
        cache_copy(g).wait()
    to_far(0)
    residents(0, 0)
    near_prefix(0)
    lax.fori_loop(1, 3, middle, 0)
    partner_prefix()
    lax.fori_loop(3, 5, middle, 0)
    far_prefix(0)
    lax.fori_loop(5, NC, middle, 0)
    lax.fori_loop(0, NC, to_z, 0)
    to_near(NC - 1)
    lax.fori_loop(NC, NPD // 4, residents, 0)
    by_step(done_res, out_res)
    near_prefix(1)
    for name in where:
        shared_pair(0, name)
    far_prefix(1)
    for name in where:
        shared_pair(1, name)

    for k in range(7):
        ssq_copy(k).wait_recv()

    for i in range(TOK // 16, (TOK + WINDOW) // 16):
        kv[i] = jnp.zeros((16, PAIR), BF16)

    def finish(c, carry):
        z2_copy(c).wait_recv()
        x_copy(0, c).wait_recv()
        x_copy(1, c).wait_recv()
        squares = lax.dot_general(
            ssq[:, c, 0, :], jnp.ones((8, HD), F32), TN,
            precision=lax.Precision.HIGHEST, preferred_element_type=F32,
        )
        inverse = lax.rsqrt(squares * (1.0 / D) + EPS)
        total = add(p00[c], z2r[c], xr[0, c], xr[1, c])
        both = jnp.concatenate([total[:, :HD] * inverse, total[:, HD:] * inverse], axis=1)
        kv[pl.ds(pl.multiple_of(c * (RB // 16), RB // 16), RB // 16)] = both.astype(BF16).reshape(RB // 16, 16, PAIR)
        return carry

    lax.fori_loop(0, NC, finish, 0)

    def drain(c, carry):
        s1_copy(c).wait_send()
        s2_copy(0, c).wait_send()
        s2_copy(1, c).wait_send()
        r2_copy(c).wait_send()
        z2_copy(c).wait_send()
        x_copy(0, c).wait_send()
        x_copy(1, c).wait_send()
        return carry

    lax.fori_loop(0, NC, drain, 0)
    for k in range(7):
        ssq_copy(k).wait_send()
    for cp in sends:
        cp.wait_send()


def by_step(rows, natural):
    for t in range(STEPS):
        for g in range(GROUP):
            natural[t, :, g * HD:(g + 1) * HD] = rows[:, t * GROUP + g, :]


def prompts(res, kv, pacc, plse, aq, astep, req_slot, req_start, lens, out_arr, out_res, done_arr, res_sem):
    copy_res = pltpu.make_async_copy(res, out_res, res_sem)
    copy_res.start()
    width = WINDOW + STEP_PAD
    key_col = lax.broadcasted_iota(jnp.int32, (ROWS, width), 1)
    key_step = lax.broadcasted_iota(jnp.int32, (ROWS, width), 0) // GROUP
    steps_valid = (key_col >= WINDOW) & (key_col - WINDOW <= key_step)

    def arrivals(i, carry):
        group = [i * 4 + k for k in range(4)]
        scores, values = [], []
        for n in group:
            start, length = req_start[n], lens[n]
            base = lax.shift_right_logical(start, 4)
            offset = lax.bitwise_and(start, 15)
            window = [kv[base + k] for k in range(WINDOW // 16)]
            keys = jnp.concatenate([piece[:, :HD] for piece in window] + [astep[0, n].astype(BF16)], axis=0)
            values.append(jnp.concatenate([piece[:, HD:] for piece in window] + [astep[1, n].astype(BF16)], axis=0))
            part = lax.dot_general(aq[n].astype(BF16), keys, NT, preferred_element_type=F32)
            valid = ((key_col >= offset) & (key_col < offset + length)) | steps_valid
            scores.append(jnp.where(valid, part, -1e30))
        slots = [req_slot[n] for n in group]
        scores = jnp.concatenate(scores, axis=0) * SCALE
        level = jnp.concatenate([plse[slot] for slot in slots], axis=0)
        highest = jnp.maximum(jnp.max(scores, axis=1, keepdims=True), level)
        raised = jnp.exp2(scores - highest[:, :width])
        before = jnp.exp2(level - highest)
        total = jnp.sum(raised, axis=1, keepdims=True) + before
        inverse = 1.0 / total
        raised = raised.astype(BF16)
        for k, n in enumerate(group):
            rows = slice(k * ROWS, (k + 1) * ROWS)
            result = jnp.dot(raised[rows], values[k], preferred_element_type=F32)
            done_arr[n] = (result + pacc[slots[k]] * before[rows]) * inverse[rows]
        return carry

    lax.fori_loop(0, NPD // 4, arrivals, 0)
    by_step(done_arr, out_arr)
    copy_res.wait()


def fused(*operands):
    vmem = pl.BlockSpec(memory_space=pltpu.VMEM)
    smem = pl.BlockSpec(memory_space=pltpu.SMEM)
    hbm = pl.BlockSpec(memory_space=pl.ANY)
    dma = pltpu.SemaphoreType.DMA
    block = pltpu.VMEM((NC, RB, PAIR), BF16)
    pair = pltpu.VMEM((2, NC, RB, PAIR), BF16)
    by_rows = pltpu.VMEM((NPD, ROWS, HD), F32)
    steps = pltpu.VMEM((2, NPD, STEP_PAD, HD), F32)
    scratch = [
        by_rows, steps, by_rows,
        pltpu.VMEM((NC, RB, WIDTH), BF16),
        pltpu.VMEM((8, WIDTH, PAIR), BF16),
        pltpu.VMEM((8, NPD // 8, CACHE, PAIR), BF16),
        [pltpu.VMEM((PREFIX, PAIR), BF16)] * (OWNERS - 1),
        block, pair, block, block, pair, block,
        block, pair, block, block, pair,
        pltpu.VMEM((8, NC, 1, RB), F32),
        pltpu.VMEM((OWNERS * CAP, ROWS, HD), F32),
        dma((NC,)), dma((8,)), dma((8,)),
        dma((NC,)), dma((NC,)), dma((2, NC)), dma((2, NC)), dma((NC,)), dma((NC,)),
        dma((NC,)), dma((NC,)), dma((2, NC)), dma((2, NC)),
        dma((7,)), dma((7,)), dma((15,)), dma((15,)),
    ]
    out = jax.ShapeDtypeStruct((STEPS, NPD, WIDTH), F32)
    slots = (OWNERS * CAP, ROWS, HD)
    numbers = jax.ShapeDtypeStruct((NPD,), jnp.int32)
    res, *rest = pl.pallas_call(
        kernel,
        out_shape=(
            out,
            jax.ShapeDtypeStruct(((TOK + WINDOW) // 16, 16, PAIR), BF16),
            jax.ShapeDtypeStruct(slots, BF16),
            jax.ShapeDtypeStruct(slots, F32),
            jax.ShapeDtypeStruct((NPD, ROWS, HD), BF16),
            jax.ShapeDtypeStruct((2, NPD, STEP_PAD, HD), BF16),
            numbers,
            numbers,
        ),
        in_specs=[hbm, vmem, hbm, smem, smem, vmem, vmem, vmem, vmem, hbm, vmem, smem],
        out_specs=(vmem,) * 6 + (smem,) * 2,
        scratch_shapes=scratch,
        compiler_params=pltpu.CompilerParams(
            collective_id=0, has_side_effects=True, vmem_limit_bytes=63 * 2**20
        ),
        cost_estimate=pl.CostEstimate(flops=18 * 10**9, bytes_accessed=30 * 10**6, transcendentals=6 * 10**6),
        name="prefill_decode",
    )(*operands)
    return pl.pallas_call(
        prompts,
        out_shape=(out, out),
        in_specs=[hbm] + [vmem] * 5 + [smem] * 3,
        out_specs=(vmem, hbm),
        scratch_shapes=[by_rows, dma],
        compiler_params=pltpu.CompilerParams(vmem_limit_bytes=63 * 2**20),
        cost_estimate=pl.CostEstimate(flops=10**8, bytes_accessed=7 * 10**6, transcendentals=3 * 10**5),
        name="prompts",
    )(res, *rest, operands[3])


def shards(
    tokens, norm_gain, kv_weight, prompt_lens, owner_of, arr_query, arr_step_kv, prefix_kv,
    res_query, res_cache, res_step_kv, cache_lens,
):
    return fused(
        tokens.reshape(NC, RB, WIDTH), norm_gain, kv_weight, prompt_lens.reshape(NPD), owner_of.reshape(NPD), arr_query, arr_step_kv,
        prefix_kv, res_query, res_cache.reshape(8, NPD // 8, CACHE, PAIR), res_step_kv, cache_lens,
    )


def solution(mesh):
    in_specs = (
        P("req", "head"),
        P("head"),
        P("head", None),
        P("req", None),
        P("req", None),
        P(None, "req", "head"),
        P(None, "req", "head"),
        P("req", "head"),
        P(None, "req", "head"),
        P("req", None, "head"),
        P(None, "req", "head"),
        P("req"),
    )
    out_specs = (P(None, "req", "head"), P(None, "req", "head"))
    return jax.shard_map(shards, mesh=mesh, in_specs=in_specs, out_specs=out_specs, check_vma=False)
```

```python
import functools
import math

import jax
import jax.numpy as jnp
from jax import lax
from jax.experimental import pallas as pl
from jax.experimental.pallas import tpu as pltpu
from jax.sharding import PartitionSpec as P

D = 16384
HD = 128
PAIR = 2 * HD
STEPS = 4
GROUP = 16
ROWS = STEPS * GROUP
TOK = 1536
WIDTH = 2048
NC = 6
RB = TOK // NC
NPD = 32
OWNERS = 16
CAP = 4
PREFIX = 1024
CACHE = 512
STEP_PAD = 16
WINDOW = 80
EPS = 1e-05
LOG2E = math.log2(math.e)
SCALE = HD**-0.5 * LOG2E
MESH = pl.DeviceIdType.MESH

ORDER = ((2, 1), (1, 1), (3, 1), (2, 0), (0, 1), (1, 0), (3, 0), (0, 0))
F32 = jnp.float32
BF16 = jnp.bfloat16
NT = (((1,), (1,)), ((), ()))
TN = (((0,), (0,)), ((), ()))


def mod(a, n):
    return lax.rem(a, n)


def kernel(
    tokens, gain, weight, lens, owner, arr_query, arr_step, prefix, res_query, cache, res_step, cache_lens,
    out_res, kv, pacc, plse, aq, astep, req_slot, req_start,
    rq, rstep, done_res,
    tok, w, cach, pre, s1, s2, p20, p01, pd, p00, s1r, s2r, r2r, z2r, xr,
    ssq, slot_query,
    tok_sem, w_sem, cache_sem,
    s1_ss, s1_rs, s2_ss, s2_rs, r2_ss, r2_rs, z2_ss, z2_rs, x_ss, x_rs,
    ssq_ss, ssq_rs, pre_ss, pre_rs,
):
    r = lax.axis_index("req")
    h = lax.axis_index("head")
    x, zl = h // 2, mod(h, 2)
    zh, y, core = r // 8, mod(r // 2, 4), mod(r, 2)

    def head_at(dx, zf):
        return mod(x + dx, 4) * 2 + mod(zl + zf, 2)

    def req_at(zx, dy, cx):
        return mod(zh + zx, 2) * 8 + mod(y + dy, 4) * 2 + mod(core + cx, 2)

    def tok_copy(c):
        return pltpu.make_async_copy(tokens.at[c], tok.at[c], tok_sem.at[c])

    def w_copy(k):
        cols = pl.ds(pl.multiple_of(head_at(*ORDER[k]) * PAIR, PAIR), PAIR)
        return pltpu.make_async_copy(weight.at[:, cols], w.at[k], w_sem.at[k])

    def cache_copy(g):
        return pltpu.make_async_copy(cache.at[g], cach.at[g], cache_sem.at[g])

    tok_copy(0).start()
    w_copy(0).start()

    barrier = pltpu.get_barrier_semaphore()
    peers = [(r, mod(h + k, 8)) for k in range(1, 8)]
    peers += [(req_at(1, 0, 0), h), (req_at(0, 1, 0), h), (req_at(0, 3, 0), h), (req_at(0, 0, 1), h)]
    for peer in peers:
        pl.semaphore_signal(barrier, inc=1, device_id=peer, device_id_type=MESH)
    pl.semaphore_wait(barrier, len(peers))

    def remote(src, dst, ss, rs, device):
        return pltpu.make_async_remote_copy(
            src_ref=src, dst_ref=dst, send_sem=ss, recv_sem=rs, device_id=device, device_id_type=MESH
        )

    turn = 1 + 2 * core
    where = {"own": 0, "back": 4 - turn, "front": turn, "far": 2}
    names = [(zx, name, cx) for zx in range(2) for name in where for cx in range(2)][1:]
    held = dict(zip(names, pre))
    held[0, "own", 0] = prefix
    sends = []

    def send_prefix(name, to_name, to):
        n = len(sends)
        cp = remote(held[name], held[to_name], pre_ss.at[n], pre_rs.at[names.index(to_name)], (req_at(*to), h))
        cp.start()
        sends.append(cp)

    def wait_prefix(name):
        n = names.index(name)
        remote(held[name], held[name], pre_ss.at[0], pre_rs.at[n], (req_at(0, 0, 1), h)).wait_recv()

    def own_prefix(zx):
        send_prefix((zx, "own", 0), (zx, "back", 0), (0, turn, 0))
        send_prefix((zx, "own", 0), (zx, "front", 0), (0, 4 - turn, 0))
        send_prefix((zx, "own", 0), (zx, "own", 1), (0, 0, 1))

    def near_prefix(zx):
        wait_prefix((zx, "back", 0))
        send_prefix((zx, "back", 0), (zx, "far", 0), (0, turn, 0))
        send_prefix((zx, "back", 0), (zx, "back", 1), (0, 0, 1))
        wait_prefix((zx, "front", 0))
        send_prefix((zx, "front", 0), (zx, "front", 1), (0, 0, 1))

    def far_prefix(zx):
        wait_prefix((zx, "far", 0))
        send_prefix((zx, "far", 0), (zx, "far", 1), (0, 0, 1))

    def partner_prefix():
        wait_prefix((1, "own", 0))
        own_prefix(1)

    send_prefix((0, "own", 0), (1, "own", 0), (1, 0, 0))
    own_prefix(0)
    for c in range(1, NC):
        tok_copy(c).start()
    for k in range(1, 8):
        w_copy(k).start()
    for g in range(8):
        cache_copy(g).start()

    z_dev = (r, head_at(0, 1))

    def x_dev(step):
        return (r, mod(x + step, 4) * 2 + zl)

    def s1_copy(c):
        return remote(s1.at[c], s1r.at[c], s1_ss.at[c], s1_rs.at[c], z_dev)

    def s2_copy(d, c):
        return remote(s2.at[d, c], s2r.at[d, c], s2_ss.at[d, c], s2_rs.at[d, c], x_dev(1 + 2 * d))

    def r2_copy(c):
        return remote(p20.at[c], r2r.at[c], r2_ss.at[c], r2_rs.at[c], x_dev(1 + 2 * mod(c, 2)))

    def z2_copy(c):
        return remote(p01.at[c], z2r.at[c], z2_ss.at[c], z2_rs.at[c], z_dev)

    def x_copy(d, c):
        return remote(pd.at[d, c], xr.at[d, c], x_ss.at[d, c], x_rs.at[d, c], x_dev(1 + 2 * d))

    def project(k, c):
        return jnp.dot(tok[c], w[k], preferred_element_type=F32).astype(BF16)

    for k in range(3):
        w_copy(k).wait()

    def first(c, carry):
        tok_copy(c).wait()
        acc = []
        for b in range(4):
            rows = slice(b * (RB // 4), (b + 1) * (RB // 4))
            total = None
            for j in range(WIDTH // HD):
                cols = slice(j * HD, (j + 1) * HD)
                part = tok[c, rows, cols].astype(F32)
                square = part * part
                total = square if total is None else total + square
                tok[c, rows, cols] = (part * gain[cols].astype(F32)[None, :]).astype(BF16)
            acc.append(total)
        total = jnp.concatenate(acc, axis=0)
        s1[c] = project(0, c)
        s1_copy(c).start()
        s2[0, c] = project(1, c)
        s2_copy(0, c).start()
        s2[1, c] = project(2, c)
        s2_copy(1, c).start()
        row = lax.dot_general(
            jnp.ones((8, HD), F32), total, NT, precision=lax.Precision.HIGHEST, preferred_element_type=F32
        )
        ssq[h, c] = row[0:1, :]
        return carry

    lax.fori_loop(0, NC, first, 0)

    def ssq_copy(k):
        return remote(ssq.at[h], ssq.at[h], ssq_ss.at[k], ssq_rs.at[k], (r, mod(h + k + 1, 8)))

    for k in range(7):
        ssq_copy(k).start()

    def by_request(n, carry):
        mine = owner[n]

        def look(m, found):
            before = (m < n).astype(jnp.int32)
            return found[0] + (owner[m] == mine).astype(jnp.int32) * before, found[1] + lens[m] * before

        rank, begin = lax.fori_loop(0, NPD, look, (jnp.int32(0), jnp.int32(0)))
        req_slot[n] = mine * CAP + rank
        req_start[n] = begin
        return carry

    def by_rows(natural, rows):
        for t in range(STEPS):
            for g in range(GROUP):
                rows[:, t * GROUP + g, :] = natural[t, :, g * HD:(g + 1) * HD].astype(rows.dtype)

    def queries_by_slot():
        lax.fori_loop(0, NPD, by_request, 0)
        request = lax.broadcasted_iota(jnp.int32, (OWNERS * CAP, NPD), 1)
        held = jnp.full((OWNERS * CAP, NPD), -1, jnp.int32)
        for n in range(NPD):
            held = jnp.where(request == n, req_slot[n], held)
        slot = lax.broadcasted_iota(jnp.int32, (OWNERS * CAP, NPD), 0)
        chosen = jnp.where(held == slot, 1.0, 0.0).astype(BF16)
        for t in range(STEPS):
            for g in range(GROUP):
                part = jnp.dot(chosen, arr_query[t, :, g * HD:(g + 1) * HD], preferred_element_type=F32)
                slot_query[:, t * GROUP + g, :] = part

    def steps_by_rows(natural, rows):
        rows[...] = jnp.zeros(rows.shape, rows.dtype)
        for t in range(STEPS):
            for half in range(2):
                rows[half, :, t, :] = natural[t, :, half * HD:(half + 1) * HD].astype(rows.dtype)

    by_rows(res_query, rq)
    steps_by_rows(res_step, rstep)
    by_rows(arr_query, aq)
    steps_by_rows(arr_step, astep)

    def add(*parts):
        return functools.reduce(jnp.add, [part.astype(F32) for part in parts])

    def straight(c, carry):
        pd[0, c] = project(5, c)
        pd[1, c] = project(6, c)
        x_copy(1 - mod(c, 2), c).start()
        return carry

    def second(c, carry):
        p20[c] = project(3, c)
        p01[c] = project(4, c)
        p00[c] = project(7, c)
        return carry

    def to_far(c):
        s1_copy(c).wait_recv()
        p20[c] = add(p20[c], s1r[c]).astype(BF16)
        r2_copy(c).start()

    def to_near(c):
        d = mod(c, 2)
        r2_copy(c).wait_recv()
        pd[d, c] = add(pd[d, c], r2r[c]).astype(BF16)
        x_copy(d, c).start()

    def to_z(c, carry):
        s2_copy(0, c).wait_recv()
        s2_copy(1, c).wait_recv()
        p01[c] = add(p01[c], s2r[0, c], s2r[1, c]).astype(BF16)
        z2_copy(c).start()
        return carry

    col = lax.broadcasted_iota(jnp.int32, (ROWS, CACHE + STEP_PAD), 1)
    row_step = lax.broadcasted_iota(jnp.int32, (ROWS, CACHE + STEP_PAD), 0) // GROUP
    recent_valid = (col >= CACHE) & (col - CACHE <= row_step)

    def residents(i, carry):
        group = [i * 4 + k for k in range(4)]
        keys, values = [
            [
                jnp.concatenate([cach[i, k, :, half * HD:(half + 1) * HD], rstep[half, n].astype(BF16)], axis=0)
                for k, n in enumerate(group)
            ]
            for half in range(2)
        ]
        scores = []
        for k, n in enumerate(group):
            part = lax.dot_general(rq[n].astype(BF16), keys[k], NT, preferred_element_type=F32)
            scores.append(jnp.where((col < cache_lens[n]) | recent_valid, part, -1e30))
        scores = jnp.concatenate(scores, axis=0)
        highest = jnp.max(scores, axis=1, keepdims=True)
        raised = jnp.exp2((scores - highest) * SCALE)
        total = jnp.sum(raised, axis=1, keepdims=True)
        raised = raised.astype(BF16)
        for k, n in enumerate(group):
            rows = slice(k * ROWS, (k + 1) * ROWS)
            result = jnp.dot(raised[rows], values[k], preferred_element_type=F32)
            done_res[n] = result / total[rows]
        return carry

    def shared(zx, name, cx):
        rows = held[zx, name, cx]
        dy = where[name] if cx == 0 else mod(4 - where[name], 4)
        slots = pl.ds(pl.multiple_of(req_at(zx, dy, cx) * CAP, CAP), CAP)
        queries = slot_query[slots].reshape(CAP * ROWS, HD).astype(BF16)
        scores = lax.dot_general(queries, rows[:, :HD], NT, preferred_element_type=F32)
        highest = jnp.max(scores, axis=1, keepdims=True)
        raised = jnp.exp2((scores - highest) * SCALE)
        total = jnp.sum(raised, axis=1, keepdims=True)
        result = jnp.dot(raised.astype(BF16), rows[:, HD:], preferred_element_type=F32) / total
        level = jnp.broadcast_to(highest * SCALE + jnp.log2(total), (CAP * ROWS, HD))
        pacc[slots] = result.astype(BF16).reshape(CAP, ROWS, HD)
        plse[slots] = level.reshape(CAP, ROWS, HD)

    def shared_pair(zx, name):
        shared(zx, name, 0)
        wait_prefix((zx, name, 1))
        shared(zx, name, 1)

    def middle(c, carry):
        to_far(c)
        to_near(c - 1)
        return residents(c, carry)

    w_copy(5).wait()
    w_copy(6).wait()
    lax.fori_loop(0, NC, straight, 0)
    w_copy(3).wait()
    w_copy(4).wait()
    w_copy(7).wait()
    lax.fori_loop(0, NC, second, 0)
    queries_by_slot()
    for g in range(8):
        cache_copy(g).wait()
    to_far(0)
    residents(0, 0)
    near_prefix(0)
    lax.fori_loop(1, 2, middle, 0)
    shared_pair(0, "own")
    lax.fori_loop(2, 3, middle, 0)
    partner_prefix()
    shared_pair(0, "back")
    lax.fori_loop(3, 4, middle, 0)
    shared_pair(0, "front")
    lax.fori_loop(4, 5, middle, 0)
    far_prefix(0)
    lax.fori_loop(5, NC, middle, 0)
    lax.fori_loop(0, NC, to_z, 0)
    to_near(NC - 1)
    shared_pair(0, "far")
    near_prefix(1)
    shared_pair(1, "own")
    lax.fori_loop(NC, NPD // 4, residents, 0)
    by_step(done_res, out_res)
    shared_pair(1, "back")
    far_prefix(1)
    shared_pair(1, "front")
    shared_pair(1, "far")

    for k in range(7):
        ssq_copy(k).wait_recv()

    for i in range(TOK // 16, (TOK + WINDOW) // 16):
        kv[i] = jnp.zeros((16, PAIR), BF16)

    def finish(c, carry):
        z2_copy(c).wait_recv()
        x_copy(0, c).wait_recv()
        x_copy(1, c).wait_recv()
        squares = lax.dot_general(
            ssq[:, c, 0, :], jnp.ones((8, HD), F32), TN,
            precision=lax.Precision.HIGHEST, preferred_element_type=F32,
        )
        inverse = lax.rsqrt(squares * (1.0 / D) + EPS)
        total = add(p00[c], z2r[c], xr[0, c], xr[1, c])
        both = jnp.concatenate([total[:, :HD] * inverse, total[:, HD:] * inverse], axis=1)
        kv[pl.ds(pl.multiple_of(c * (RB // 16), RB // 16), RB // 16)] = both.astype(BF16).reshape(RB // 16, 16, PAIR)
        return carry

    lax.fori_loop(0, NC, finish, 0)

    def drain(c, carry):
        s1_copy(c).wait_send()
        s2_copy(0, c).wait_send()
        s2_copy(1, c).wait_send()
        r2_copy(c).wait_send()
        z2_copy(c).wait_send()
        x_copy(0, c).wait_send()
        x_copy(1, c).wait_send()
        return carry

    lax.fori_loop(0, NC, drain, 0)
    for k in range(7):
        ssq_copy(k).wait_send()
    for cp in sends:
        cp.wait_send()


def by_step(rows, natural):
    for t in range(STEPS):
        for g in range(GROUP):
            natural[t, :, g * HD:(g + 1) * HD] = rows[:, t * GROUP + g, :]


def prompts(res, kv, pacc, plse, aq, astep, req_slot, req_start, lens, out_arr, out_res, done_arr):
    out_res[...] = res[...]
    width = WINDOW + STEP_PAD
    key_col = lax.broadcasted_iota(jnp.int32, (ROWS, width), 1)
    key_step = lax.broadcasted_iota(jnp.int32, (ROWS, width), 0) // GROUP
    steps_valid = (key_col >= WINDOW) & (key_col - WINDOW <= key_step)

    def arrivals(i, carry):
        group = [i * 4 + k for k in range(4)]
        scores, values = [], []
        for n in group:
            start, length = req_start[n], lens[n]
            base = lax.shift_right_logical(start, 4)
            offset = lax.bitwise_and(start, 15)
            window = [kv[base + k] for k in range(WINDOW // 16)]
            keys = jnp.concatenate([piece[:, :HD] for piece in window] + [astep[0, n].astype(BF16)], axis=0)
            values.append(jnp.concatenate([piece[:, HD:] for piece in window] + [astep[1, n].astype(BF16)], axis=0))
            part = lax.dot_general(aq[n].astype(BF16), keys, NT, preferred_element_type=F32)
            valid = ((key_col >= offset) & (key_col < offset + length)) | steps_valid
            scores.append(jnp.where(valid, part, -1e30))
        slots = [req_slot[n] for n in group]
        scores = jnp.concatenate(scores, axis=0) * SCALE
        level = jnp.concatenate([plse[slot] for slot in slots], axis=0)
        highest = jnp.maximum(jnp.max(scores, axis=1, keepdims=True), level)
        raised = jnp.exp2(scores - highest[:, :width])
        before = jnp.exp2(level - highest)
        total = jnp.sum(raised, axis=1, keepdims=True) + before
        inverse = 1.0 / total
        raised = raised.astype(BF16)
        for k, n in enumerate(group):
            rows = slice(k * ROWS, (k + 1) * ROWS)
            result = jnp.dot(raised[rows], values[k], preferred_element_type=F32)
            done_arr[n] = (result + pacc[slots[k]] * before[rows]) * inverse[rows]
        return carry

    lax.fori_loop(0, NPD // 4, arrivals, 0)
    by_step(done_arr, out_arr)


def fused(*operands):
    vmem = pl.BlockSpec(memory_space=pltpu.VMEM)
    smem = pl.BlockSpec(memory_space=pltpu.SMEM)
    hbm = pl.BlockSpec(memory_space=pl.ANY)
    dma = pltpu.SemaphoreType.DMA
    block = pltpu.VMEM((NC, RB, PAIR), BF16)
    pair = pltpu.VMEM((2, NC, RB, PAIR), BF16)
    by_rows = pltpu.VMEM((NPD, ROWS, HD), F32)
    steps = pltpu.VMEM((2, NPD, STEP_PAD, HD), F32)
    scratch = [
        by_rows, steps, by_rows,
        pltpu.VMEM((NC, RB, WIDTH), BF16),
        pltpu.VMEM((8, WIDTH, PAIR), BF16),
        pltpu.VMEM((8, NPD // 8, CACHE, PAIR), BF16),
        [pltpu.VMEM((PREFIX, PAIR), BF16)] * (OWNERS - 1),
        block, pair, block, block, pair, block,
        block, pair, block, block, pair,
        pltpu.VMEM((8, NC, 1, RB), F32),
        pltpu.VMEM((OWNERS * CAP, ROWS, HD), F32),
        dma((NC,)), dma((8,)), dma((8,)),
        dma((NC,)), dma((NC,)), dma((2, NC)), dma((2, NC)), dma((NC,)), dma((NC,)),
        dma((NC,)), dma((NC,)), dma((2, NC)), dma((2, NC)),
        dma((7,)), dma((7,)), dma((15,)), dma((15,)),
    ]
    out = jax.ShapeDtypeStruct((STEPS, NPD, WIDTH), F32)
    slots = (OWNERS * CAP, ROWS, HD)
    numbers = jax.ShapeDtypeStruct((NPD,), jnp.int32)
    res, *rest = pl.pallas_call(
        kernel,
        out_shape=(
            out,
            jax.ShapeDtypeStruct(((TOK + WINDOW) // 16, 16, PAIR), BF16),
            jax.ShapeDtypeStruct(slots, BF16),
            jax.ShapeDtypeStruct(slots, F32),
            jax.ShapeDtypeStruct((NPD, ROWS, HD), BF16),
            jax.ShapeDtypeStruct((2, NPD, STEP_PAD, HD), BF16),
            numbers,
            numbers,
        ),
        in_specs=[hbm, vmem, hbm, smem, smem, vmem, vmem, vmem, vmem, hbm, vmem, smem],
        out_specs=(vmem,) * 6 + (smem,) * 2,
        scratch_shapes=scratch,
        compiler_params=pltpu.CompilerParams(
            collective_id=0, has_side_effects=True, vmem_limit_bytes=63 * 2**20
        ),
        cost_estimate=pl.CostEstimate(flops=18 * 10**9, bytes_accessed=30 * 10**6, transcendentals=6 * 10**6),
        name="prefill_decode",
    )(*operands)
    return pl.pallas_call(
        prompts,
        out_shape=(out, out),
        in_specs=[vmem] * 6 + [smem] * 3,
        out_specs=(vmem, vmem),
        scratch_shapes=[by_rows],
        compiler_params=pltpu.CompilerParams(vmem_limit_bytes=63 * 2**20),
        cost_estimate=pl.CostEstimate(flops=10**8, bytes_accessed=7 * 10**6, transcendentals=3 * 10**5),
        name="prompts",
    )(res, *rest, operands[3])


def shards(
    tokens, norm_gain, kv_weight, prompt_lens, owner_of, arr_query, arr_step_kv, prefix_kv,
    res_query, res_cache, res_step_kv, cache_lens,
):
    return fused(
        tokens.reshape(NC, RB, WIDTH), norm_gain, kv_weight, prompt_lens.reshape(NPD), owner_of.reshape(NPD), arr_query, arr_step_kv,
        prefix_kv, res_query, res_cache.reshape(8, NPD // 8, CACHE, PAIR), res_step_kv, cache_lens,
    )


def solution(mesh):
    in_specs = (
        P("req", "head"),
        P("head"),
        P("head", None),
        P("req", None),
        P("req", None),
        P(None, "req", "head"),
        P(None, "req", "head"),
        P("req", "head"),
        P(None, "req", "head"),
        P("req", None, "head"),
        P(None, "req", "head"),
        P("req"),
    )
    out_specs = (P(None, "req", "head"), P(None, "req", "head"))
    return jax.shard_map(shards, mesh=mesh, in_specs=in_specs, out_specs=out_specs, check_vma=False)
```

```python
import functools
import math

import jax
import jax.numpy as jnp
from jax import lax
from jax.experimental import pallas as pl
from jax.experimental.pallas import tpu as pltpu
from jax.sharding import PartitionSpec as P

D = 16384
HD = 128
PAIR = 2 * HD
STEPS = 4
GROUP = 16
ROWS = STEPS * GROUP
TOK = 1536
WIDTH = 2048
NC = 6
RB = TOK // NC
NPD = 32
OWNERS = 16
CAP = 4
PREFIX = 1024
CACHE = 512
STEP_PAD = 16
WINDOW = 80
EPS = 1e-05
LOG2E = math.log2(math.e)
SCALE = HD**-0.5 * LOG2E
MESH = pl.DeviceIdType.MESH

ORDER = ((2, 1), (1, 1), (3, 1), (2, 0), (0, 1), (1, 0), (3, 0), (0, 0))
F32 = jnp.float32
BF16 = jnp.bfloat16
NT = (((1,), (1,)), ((), ()))
TN = (((0,), (0,)), ((), ()))


def mod(a, n):
    return lax.rem(a, n)


def kernel(
    tokens, gain, weight, lens, owner, arr_query, arr_step, prefix, res_query, cache, res_step, cache_lens,
    out_res, kv, pacc, plse, aq, astep, req_slot, req_start,
    rq, rstep, done_res,
    tok, w, cach, pre, s1, s2, p20, p01, pd, p00, s1r, s2r, r2r, z2r, xr,
    ssq, slot_query,
    tok_sem, w_sem, cache_sem,
    s1_ss, s1_rs, s2_ss, s2_rs, r2_ss, r2_rs, z2_ss, z2_rs, x_ss, x_rs,
    ssq_ss, ssq_rs, pre_ss, pre_rs,
):
    r = lax.axis_index("req")
    h = lax.axis_index("head")
    x, zl = h // 2, mod(h, 2)
    zh, y, core = r // 8, mod(r // 2, 4), mod(r, 2)

    def head_at(dx, zf):
        return mod(x + dx, 4) * 2 + mod(zl + zf, 2)

    def req_at(zx, dy, cx):
        return mod(zh + zx, 2) * 8 + mod(y + dy, 4) * 2 + mod(core + cx, 2)

    def tok_copy(c):
        return pltpu.make_async_copy(tokens.at[c], tok.at[c], tok_sem.at[c])

    def w_copy(k):
        cols = pl.ds(pl.multiple_of(head_at(*ORDER[k]) * PAIR, PAIR), PAIR)
        return pltpu.make_async_copy(weight.at[:, cols], w.at[k], w_sem.at[k])

    def cache_copy(g):
        return pltpu.make_async_copy(cache.at[g], cach.at[g], cache_sem.at[g])

    tok_copy(0).start()
    w_copy(0).start()

    barrier = pltpu.get_barrier_semaphore()
    peers = [(r, mod(h + k, 8)) for k in range(1, 8)]
    peers += [(req_at(1, 0, 0), h), (req_at(0, 1, 0), h), (req_at(0, 3, 0), h), (req_at(0, 0, 1), h)]
    for peer in peers:
        pl.semaphore_signal(barrier, inc=1, device_id=peer, device_id_type=MESH)
    pl.semaphore_wait(barrier, len(peers))

    def remote(src, dst, ss, rs, device):
        return pltpu.make_async_remote_copy(
            src_ref=src, dst_ref=dst, send_sem=ss, recv_sem=rs, device_id=device, device_id_type=MESH
        )

    turn = 1 + 2 * core
    where = {"own": 0, "back": 4 - turn, "front": turn, "far": 2}
    names = [(zx, name, cx) for zx in range(2) for name in where for cx in range(2)][1:]
    held = dict(zip(names, pre))
    held[0, "own", 0] = prefix
    sends = []

    def send_prefix(name, to_name, to):
        n = len(sends)
        cp = remote(held[name], held[to_name], pre_ss.at[n], pre_rs.at[names.index(to_name)], (req_at(*to), h))
        cp.start()
        sends.append(cp)

    def wait_prefix(name):
        n = names.index(name)
        remote(held[name], held[name], pre_ss.at[0], pre_rs.at[n], (req_at(0, 0, 1), h)).wait_recv()

    def own_prefix(zx):
        send_prefix((zx, "own", 0), (zx, "back", 0), (0, turn, 0))
        send_prefix((zx, "own", 0), (zx, "front", 0), (0, 4 - turn, 0))
        send_prefix((zx, "own", 0), (zx, "own", 1), (0, 0, 1))

    def near_prefix(zx):
        wait_prefix((zx, "back", 0))
        send_prefix((zx, "back", 0), (zx, "far", 0), (0, turn, 0))
        send_prefix((zx, "back", 0), (zx, "back", 1), (0, 0, 1))
        wait_prefix((zx, "front", 0))
        send_prefix((zx, "front", 0), (zx, "front", 1), (0, 0, 1))

    def far_prefix(zx):
        wait_prefix((zx, "far", 0))
        send_prefix((zx, "far", 0), (zx, "far", 1), (0, 0, 1))

    def partner_prefix():
        wait_prefix((1, "own", 0))
        own_prefix(1)

    send_prefix((0, "own", 0), (1, "own", 0), (1, 0, 0))
    own_prefix(0)
    for c in range(1, NC):
        tok_copy(c).start()
    for k in range(1, 8):
        w_copy(k).start()
    for g in range(8):
        cache_copy(g).start()

    z_dev = (r, head_at(0, 1))

    def x_dev(step):
        return (r, mod(x + step, 4) * 2 + zl)

    def s1_copy(c):
        return remote(s1.at[c], s1r.at[c], s1_ss.at[c], s1_rs.at[c], z_dev)

    def s2_copy(d, c):
        return remote(s2.at[d, c], s2r.at[d, c], s2_ss.at[d, c], s2_rs.at[d, c], x_dev(1 + 2 * d))

    def r2_copy(c):
        return remote(p20.at[c], r2r.at[c], r2_ss.at[c], r2_rs.at[c], x_dev(1 + 2 * mod(c, 2)))

    def z2_copy(c):
        return remote(p01.at[c], z2r.at[c], z2_ss.at[c], z2_rs.at[c], z_dev)

    def x_copy(d, c):
        return remote(pd.at[d, c], xr.at[d, c], x_ss.at[d, c], x_rs.at[d, c], x_dev(1 + 2 * d))

    def project(k, c):
        return jnp.dot(tok[c], w[k], preferred_element_type=F32).astype(BF16)

    for k in range(3):
        w_copy(k).wait()

    def first(c, carry):
        tok_copy(c).wait()
        acc = []
        for b in range(4):
            rows = slice(b * (RB // 4), (b + 1) * (RB // 4))
            total = None
            for j in range(WIDTH // HD):
                cols = slice(j * HD, (j + 1) * HD)
                part = tok[c, rows, cols].astype(F32)
                square = part * part
                total = square if total is None else total + square
                tok[c, rows, cols] = (part * gain[cols].astype(F32)[None, :]).astype(BF16)
            acc.append(total)
        total = jnp.concatenate(acc, axis=0)
        s1[c] = project(0, c)
        s1_copy(c).start()
        s2[0, c] = project(1, c)
        s2_copy(0, c).start()
        s2[1, c] = project(2, c)
        s2_copy(1, c).start()
        row = lax.dot_general(
            jnp.ones((8, HD), F32), total, NT, precision=lax.Precision.HIGHEST, preferred_element_type=F32
        )
        ssq[h, c] = row[0:1, :]
        return carry

    lax.fori_loop(0, NC, first, 0)

    def ssq_copy(k):
        return remote(ssq.at[h], ssq.at[h], ssq_ss.at[k], ssq_rs.at[k], (r, mod(h + k + 1, 8)))

    for k in range(7):
        ssq_copy(k).start()

    def by_request(n, carry):
        mine = owner[n]

        def look(m, found):
            before = (m < n).astype(jnp.int32)
            return found[0] + (owner[m] == mine).astype(jnp.int32) * before, found[1] + lens[m] * before

        rank, begin = lax.fori_loop(0, NPD, look, (jnp.int32(0), jnp.int32(0)))
        req_slot[n] = mine * CAP + rank
        req_start[n] = begin
        return carry

    def by_rows(natural, rows):
        for t in range(STEPS):
            for g in range(GROUP):
                rows[:, t * GROUP + g, :] = natural[t, :, g * HD:(g + 1) * HD].astype(rows.dtype)

    def queries_by_slot():
        lax.fori_loop(0, NPD, by_request, 0)
        request = lax.broadcasted_iota(jnp.int32, (OWNERS * CAP, NPD), 1)
        held = jnp.full((OWNERS * CAP, NPD), -1, jnp.int32)
        for n in range(NPD):
            held = jnp.where(request == n, req_slot[n], held)
        slot = lax.broadcasted_iota(jnp.int32, (OWNERS * CAP, NPD), 0)
        chosen = jnp.where(held == slot, 1.0, 0.0).astype(BF16)
        for t in range(STEPS):
            for g in range(GROUP):
                part = jnp.dot(chosen, arr_query[t, :, g * HD:(g + 1) * HD], preferred_element_type=F32)
                slot_query[:, t * GROUP + g, :] = part

    def steps_by_rows(natural, rows):
        rows[...] = jnp.zeros(rows.shape, rows.dtype)
        for t in range(STEPS):
            for half in range(2):
                rows[half, :, t, :] = natural[t, :, half * HD:(half + 1) * HD].astype(rows.dtype)

    def add(*parts):
        return functools.reduce(jnp.add, [part.astype(F32) for part in parts])

    def straight(c, carry):
        pd[0, c] = project(5, c)
        pd[1, c] = project(6, c)
        x_copy(1 - mod(c, 2), c).start()
        return carry

    def second(c, carry):
        p20[c] = project(3, c)
        return carry

    def third(c, carry):
        p01[c] = project(4, c)
        p00[c] = project(7, c)
        return carry

    def to_far(c):
        s1_copy(c).wait_recv()
        p20[c] = add(p20[c], s1r[c]).astype(BF16)
        r2_copy(c).start()

    def to_near(c):
        d = mod(c, 2)
        r2_copy(c).wait_recv()
        pd[d, c] = add(pd[d, c], r2r[c]).astype(BF16)
        x_copy(d, c).start()

    def to_z(c, carry):
        s2_copy(0, c).wait_recv()
        s2_copy(1, c).wait_recv()
        p01[c] = add(p01[c], s2r[0, c], s2r[1, c]).astype(BF16)
        z2_copy(c).start()
        return carry

    col = lax.broadcasted_iota(jnp.int32, (ROWS, CACHE + STEP_PAD), 1)
    row_step = lax.broadcasted_iota(jnp.int32, (ROWS, CACHE + STEP_PAD), 0) // GROUP
    recent_valid = (col >= CACHE) & (col - CACHE <= row_step)

    def residents(i, carry):
        group = [i * 4 + k for k in range(4)]
        keys, values = [
            [
                jnp.concatenate([cach[i, k, :, half * HD:(half + 1) * HD], rstep[half, n].astype(BF16)], axis=0)
                for k, n in enumerate(group)
            ]
            for half in range(2)
        ]
        scores = []
        for k, n in enumerate(group):
            part = lax.dot_general(rq[n].astype(BF16), keys[k], NT, preferred_element_type=F32)
            scores.append(jnp.where((col < cache_lens[n]) | recent_valid, part, -1e30))
        scores = jnp.concatenate(scores, axis=0)
        highest = jnp.max(scores, axis=1, keepdims=True)
        raised = jnp.exp2((scores - highest) * SCALE)
        total = jnp.sum(raised, axis=1, keepdims=True)
        raised = raised.astype(BF16)
        for k, n in enumerate(group):
            rows = slice(k * ROWS, (k + 1) * ROWS)
            result = jnp.dot(raised[rows], values[k], preferred_element_type=F32)
            done_res[n] = result / total[rows]
        return carry

    def shared(zx, name, cx):
        rows = held[zx, name, cx]
        dy = where[name] if cx == 0 else mod(4 - where[name], 4)
        slots = pl.ds(pl.multiple_of(req_at(zx, dy, cx) * CAP, CAP), CAP)
        queries = slot_query[slots].reshape(CAP * ROWS, HD).astype(BF16)
        scores = lax.dot_general(queries, rows[:, :HD], NT, preferred_element_type=F32)
        highest = jnp.max(scores, axis=1, keepdims=True)
        raised = jnp.exp2((scores - highest) * SCALE)
        total = jnp.sum(raised, axis=1, keepdims=True)
        result = jnp.dot(raised.astype(BF16), rows[:, HD:], preferred_element_type=F32) / total
        level = jnp.broadcast_to(highest * SCALE + jnp.log2(total), (CAP * ROWS, HD))
        pacc[slots] = result.astype(BF16).reshape(CAP, ROWS, HD)
        plse[slots] = level.reshape(CAP, ROWS, HD)

    def shared_pair(zx, name):
        shared(zx, name, 0)
        wait_prefix((zx, name, 1))
        shared(zx, name, 1)

    def middle(c, carry):
        to_far(c)
        to_near(c - 1)
        return residents(c, carry)

    w_copy(5).wait()
    w_copy(6).wait()
    lax.fori_loop(0, NC, straight, 0)
    w_copy(3).wait()
    lax.fori_loop(0, NC, second, 0)
    to_far(0)
    by_rows(res_query, rq)
    steps_by_rows(res_step, rstep)
    near_prefix(0)
    for g in range(8):
        cache_copy(g).wait()
    lax.fori_loop(1, 2, middle, 0)
    queries_by_slot()
    lax.fori_loop(2, 3, middle, 0)
    partner_prefix()
    w_copy(4).wait()
    w_copy(7).wait()
    lax.fori_loop(0, NC, third, 0)
    lax.fori_loop(3, 4, middle, 0)
    shared_pair(0, "own")
    lax.fori_loop(4, 5, middle, 0)
    far_prefix(0)
    shared_pair(0, "back")
    lax.fori_loop(5, NC, middle, 0)
    lax.fori_loop(0, NC, to_z, 0)
    to_near(NC - 1)
    shared_pair(0, "front")
    near_prefix(1)
    shared_pair(0, "far")
    shared_pair(1, "own")
    residents(0, 0)
    lax.fori_loop(NC, NPD // 4, residents, 0)
    by_step(done_res, out_res)
    shared_pair(1, "back")
    far_prefix(1)
    by_rows(arr_query, aq)
    steps_by_rows(arr_step, astep)
    shared_pair(1, "front")
    shared_pair(1, "far")

    for k in range(7):
        ssq_copy(k).wait_recv()

    for i in range(TOK // 16, (TOK + WINDOW) // 16):
        kv[i] = jnp.zeros((16, PAIR), BF16)

    def finish(c, carry):
        z2_copy(c).wait_recv()
        x_copy(0, c).wait_recv()
        x_copy(1, c).wait_recv()
        squares = lax.dot_general(
            ssq[:, c, 0, :], jnp.ones((8, HD), F32), TN,
            precision=lax.Precision.HIGHEST, preferred_element_type=F32,
        )
        inverse = lax.rsqrt(squares * (1.0 / D) + EPS)
        total = add(p00[c], z2r[c], xr[0, c], xr[1, c])
        both = jnp.concatenate([total[:, :HD] * inverse, total[:, HD:] * inverse], axis=1)
        kv[pl.ds(pl.multiple_of(c * (RB // 16), RB // 16), RB // 16)] = both.astype(BF16).reshape(RB // 16, 16, PAIR)
        return carry

    lax.fori_loop(0, NC, finish, 0)

    def drain(c, carry):
        s1_copy(c).wait_send()
        s2_copy(0, c).wait_send()
        s2_copy(1, c).wait_send()
        r2_copy(c).wait_send()
        z2_copy(c).wait_send()
        x_copy(0, c).wait_send()
        x_copy(1, c).wait_send()
        return carry

    lax.fori_loop(0, NC, drain, 0)
    for k in range(7):
        ssq_copy(k).wait_send()
    for cp in sends:
        cp.wait_send()


def by_step(rows, natural):
    for t in range(STEPS):
        for g in range(GROUP):
            natural[t, :, g * HD:(g + 1) * HD] = rows[:, t * GROUP + g, :]


def prompts(res, kv, pacc, plse, aq, astep, req_slot, req_start, lens, out_arr, out_res, done_arr):
    out_res[...] = res[...]
    width = WINDOW + STEP_PAD
    key_col = lax.broadcasted_iota(jnp.int32, (ROWS, width), 1)
    key_step = lax.broadcasted_iota(jnp.int32, (ROWS, width), 0) // GROUP
    steps_valid = (key_col >= WINDOW) & (key_col - WINDOW <= key_step)

    def arrivals(i, carry):
        group = [i * 4 + k for k in range(4)]
        scores, values = [], []
        for n in group:
            start, length = req_start[n], lens[n]
            base = lax.shift_right_logical(start, 4)
            offset = lax.bitwise_and(start, 15)
            window = [kv[base + k] for k in range(WINDOW // 16)]
            keys = jnp.concatenate([piece[:, :HD] for piece in window] + [astep[0, n].astype(BF16)], axis=0)
            values.append(jnp.concatenate([piece[:, HD:] for piece in window] + [astep[1, n].astype(BF16)], axis=0))
            part = lax.dot_general(aq[n].astype(BF16), keys, NT, preferred_element_type=F32)
            valid = ((key_col >= offset) & (key_col < offset + length)) | steps_valid
            scores.append(jnp.where(valid, part, -1e30))
        slots = [req_slot[n] for n in group]
        scores = jnp.concatenate(scores, axis=0) * SCALE
        level = jnp.concatenate([plse[slot] for slot in slots], axis=0)
        highest = jnp.maximum(jnp.max(scores, axis=1, keepdims=True), level)
        raised = jnp.exp2(scores - highest[:, :width])
        before = jnp.exp2(level - highest)
        total = jnp.sum(raised, axis=1, keepdims=True) + before
        inverse = 1.0 / total
        raised = raised.astype(BF16)
        for k, n in enumerate(group):
            rows = slice(k * ROWS, (k + 1) * ROWS)
            result = jnp.dot(raised[rows], values[k], preferred_element_type=F32)
            done_arr[n] = (result + pacc[slots[k]] * before[rows]) * inverse[rows]
        return carry

    lax.fori_loop(0, NPD // 4, arrivals, 0)
    by_step(done_arr, out_arr)


def fused(*operands):
    vmem = pl.BlockSpec(memory_space=pltpu.VMEM)
    smem = pl.BlockSpec(memory_space=pltpu.SMEM)
    hbm = pl.BlockSpec(memory_space=pl.ANY)
    dma = pltpu.SemaphoreType.DMA
    block = pltpu.VMEM((NC, RB, PAIR), BF16)
    pair = pltpu.VMEM((2, NC, RB, PAIR), BF16)
    by_rows = pltpu.VMEM((NPD, ROWS, HD), F32)
    steps = pltpu.VMEM((2, NPD, STEP_PAD, HD), F32)
    scratch = [
        by_rows, steps, by_rows,
        pltpu.VMEM((NC, RB, WIDTH), BF16),
        pltpu.VMEM((8, WIDTH, PAIR), BF16),
        pltpu.VMEM((8, NPD // 8, CACHE, PAIR), BF16),
        [pltpu.VMEM((PREFIX, PAIR), BF16)] * (OWNERS - 1),
        block, pair, block, block, pair, block,
        block, pair, block, block, pair,
        pltpu.VMEM((8, NC, 1, RB), F32),
        pltpu.VMEM((OWNERS * CAP, ROWS, HD), F32),
        dma((NC,)), dma((8,)), dma((8,)),
        dma((NC,)), dma((NC,)), dma((2, NC)), dma((2, NC)), dma((NC,)), dma((NC,)),
        dma((NC,)), dma((NC,)), dma((2, NC)), dma((2, NC)),
        dma((7,)), dma((7,)), dma((15,)), dma((15,)),
    ]
    out = jax.ShapeDtypeStruct((STEPS, NPD, WIDTH), F32)
    slots = (OWNERS * CAP, ROWS, HD)
    numbers = jax.ShapeDtypeStruct((NPD,), jnp.int32)
    res, *rest = pl.pallas_call(
        kernel,
        out_shape=(
            out,
            jax.ShapeDtypeStruct(((TOK + WINDOW) // 16, 16, PAIR), BF16),
            jax.ShapeDtypeStruct(slots, BF16),
            jax.ShapeDtypeStruct(slots, F32),
            jax.ShapeDtypeStruct((NPD, ROWS, HD), BF16),
            jax.ShapeDtypeStruct((2, NPD, STEP_PAD, HD), BF16),
            numbers,
            numbers,
        ),
        in_specs=[hbm, vmem, hbm, smem, smem, vmem, vmem, vmem, vmem, hbm, vmem, smem],
        out_specs=(vmem,) * 6 + (smem,) * 2,
        scratch_shapes=scratch,
        compiler_params=pltpu.CompilerParams(
            collective_id=0, has_side_effects=True, vmem_limit_bytes=63 * 2**20
        ),
        cost_estimate=pl.CostEstimate(flops=18 * 10**9, bytes_accessed=30 * 10**6, transcendentals=6 * 10**6),
        name="prefill_decode",
    )(*operands)
    return pl.pallas_call(
        prompts,
        out_shape=(out, out),
        in_specs=[vmem] * 6 + [smem] * 3,
        out_specs=(vmem, vmem),
        scratch_shapes=[by_rows],
        compiler_params=pltpu.CompilerParams(vmem_limit_bytes=63 * 2**20),
        cost_estimate=pl.CostEstimate(flops=10**8, bytes_accessed=7 * 10**6, transcendentals=3 * 10**5),
        name="prompts",
    )(res, *rest, operands[3])


def shards(
    tokens, norm_gain, kv_weight, prompt_lens, owner_of, arr_query, arr_step_kv, prefix_kv,
    res_query, res_cache, res_step_kv, cache_lens,
):
    return fused(
        tokens.reshape(NC, RB, WIDTH), norm_gain, kv_weight, prompt_lens.reshape(NPD), owner_of.reshape(NPD), arr_query, arr_step_kv,
        prefix_kv, res_query, res_cache.reshape(8, NPD // 8, CACHE, PAIR), res_step_kv, cache_lens,
    )


def solution(mesh):
    in_specs = (
        P("req", "head"),
        P("head"),
        P("head", None),
        P("req", None),
        P("req", None),
        P(None, "req", "head"),
        P(None, "req", "head"),
        P("req", "head"),
        P(None, "req", "head"),
        P("req", None, "head"),
        P(None, "req", "head"),
        P("req"),
    )
    out_specs = (P(None, "req", "head"), P(None, "req", "head"))
    return jax.shard_map(shards, mesh=mesh, in_specs=in_specs, out_specs=out_specs, check_vma=False)
```

```python
import functools
import math

import jax
import jax.numpy as jnp
from jax import lax
from jax.experimental import pallas as pl
from jax.experimental.pallas import tpu as pltpu
from jax.sharding import PartitionSpec as P

D = 16384
HD = 128
PAIR = 2 * HD
STEPS = 4
GROUP = 16
ROWS = STEPS * GROUP
TOK = 1536
WIDTH = 2048
NC = 6
RB = TOK // NC
NPD = 32
OWNERS = 16
CAP = 4
PREFIX = 1024
CACHE = 512
STEP_PAD = 16
WINDOW = 80
EPS = 1e-05
LOG2E = math.log2(math.e)
SCALE = HD**-0.5 * LOG2E
MESH = pl.DeviceIdType.MESH

ORDER = ((2, 1), (1, 1), (3, 1), (2, 0), (0, 1), (1, 0), (3, 0), (0, 0))
F32 = jnp.float32
BF16 = jnp.bfloat16
NT = (((1,), (1,)), ((), ()))
TN = (((0,), (0,)), ((), ()))


def mod(a, n):
    return lax.rem(a, n)


def kernel(
    tokens, gain, weight, lens, owner, arr_query, arr_step, prefix, res_query, cache, res_step, cache_lens,
    out_res, kv, pacc, plse, aq, astep, req_slot, req_start,
    rq, rstep, done_res,
    tok, w, cach, pre, s1, s2, p20, p01, pd, p00, s1r, s2r, r2r, z2r, xr,
    ssq, slot_query,
    tok_sem, w_sem, cache_sem,
    s1_ss, s1_rs, s2_ss, s2_rs, r2_ss, r2_rs, z2_ss, z2_rs, x_ss, x_rs,
    ssq_ss, ssq_rs, pre_ss, pre_rs,
):
    r = lax.axis_index("req")
    h = lax.axis_index("head")
    x, zl = h // 2, mod(h, 2)
    zh, y, core = r // 8, mod(r // 2, 4), mod(r, 2)

    def head_at(dx, zf):
        return mod(x + dx, 4) * 2 + mod(zl + zf, 2)

    def req_at(zx, dy, cx):
        return mod(zh + zx, 2) * 8 + mod(y + dy, 4) * 2 + mod(core + cx, 2)

    def tok_copy(c):
        return pltpu.make_async_copy(tokens.at[c], tok.at[c], tok_sem.at[c])

    def w_copy(k):
        cols = pl.ds(pl.multiple_of(head_at(*ORDER[k]) * PAIR, PAIR), PAIR)
        return pltpu.make_async_copy(weight.at[:, cols], w.at[k], w_sem.at[k])

    def cache_copy(g):
        return pltpu.make_async_copy(cache.at[g], cach.at[g], cache_sem.at[g])

    tok_copy(0).start()
    w_copy(0).start()

    barrier = pltpu.get_barrier_semaphore()
    peers = [(r, mod(h + k, 8)) for k in range(1, 8)]
    peers += [(req_at(1, 0, 0), h), (req_at(0, 1, 0), h), (req_at(0, 3, 0), h), (req_at(0, 0, 1), h)]
    for peer in peers:
        pl.semaphore_signal(barrier, inc=1, device_id=peer, device_id_type=MESH)
    pl.semaphore_wait(barrier, len(peers))

    def remote(src, dst, ss, rs, device):
        return pltpu.make_async_remote_copy(
            src_ref=src, dst_ref=dst, send_sem=ss, recv_sem=rs, device_id=device, device_id_type=MESH
        )

    turn = 1 + 2 * core
    where = {"own": 0, "back": 4 - turn, "front": turn, "far": 2}
    names = [(zx, name, cx) for zx in range(2) for name in where for cx in range(2)][1:]
    held = dict(zip(names, pre))
    held[0, "own", 0] = prefix
    sends = []

    def send_prefix(name, to_name, to):
        n = len(sends)
        cp = remote(held[name], held[to_name], pre_ss.at[n], pre_rs.at[names.index(to_name)], (req_at(*to), h))
        cp.start()
        sends.append(cp)

    def wait_prefix(name):
        n = names.index(name)
        remote(held[name], held[name], pre_ss.at[0], pre_rs.at[n], (req_at(0, 0, 1), h)).wait_recv()

    def own_prefix(zx):
        send_prefix((zx, "own", 0), (zx, "back", 0), (0, turn, 0))
        send_prefix((zx, "own", 0), (zx, "front", 0), (0, 4 - turn, 0))
        send_prefix((zx, "own", 0), (zx, "own", 1), (0, 0, 1))

    def near_prefix(zx):
        wait_prefix((zx, "back", 0))
        send_prefix((zx, "back", 0), (zx, "far", 0), (0, turn, 0))
        send_prefix((zx, "back", 0), (zx, "back", 1), (0, 0, 1))
        wait_prefix((zx, "front", 0))
        send_prefix((zx, "front", 0), (zx, "front", 1), (0, 0, 1))

    def far_prefix(zx):
        wait_prefix((zx, "far", 0))
        send_prefix((zx, "far", 0), (zx, "far", 1), (0, 0, 1))

    def partner_prefix():
        wait_prefix((1, "own", 0))
        own_prefix(1)

    send_prefix((0, "own", 0), (1, "own", 0), (1, 0, 0))
    own_prefix(0)
    for c in range(1, NC):
        tok_copy(c).start()
    for k in range(1, 8):
        w_copy(k).start()
    for g in range(8):
        cache_copy(g).start()

    z_dev = (r, head_at(0, 1))

    def x_dev(step):
        return (r, mod(x + step, 4) * 2 + zl)

    def s1_copy(c):
        return remote(s1.at[c], s1r.at[c], s1_ss.at[c], s1_rs.at[c], z_dev)

    def s2_copy(d, c):
        return remote(s2.at[d, c], s2r.at[d, c], s2_ss.at[d, c], s2_rs.at[d, c], x_dev(1 + 2 * d))

    def r2_copy(c):
        return remote(p20.at[c], r2r.at[c], r2_ss.at[c], r2_rs.at[c], x_dev(1 + 2 * mod(c, 2)))

    def z2_copy(c):
        return remote(p01.at[c], z2r.at[c], z2_ss.at[c], z2_rs.at[c], z_dev)

    def x_copy(d, c):
        return remote(pd.at[d, c], xr.at[d, c], x_ss.at[d, c], x_rs.at[d, c], x_dev(1 + 2 * d))

    def project(k, c):
        return jnp.dot(tok[c], w[k], preferred_element_type=F32).astype(BF16)

    for k in range(3):
        w_copy(k).wait()

    def first(c, carry):
        tok_copy(c).wait()
        acc = []
        for b in range(4):
            rows = slice(b * (RB // 4), (b + 1) * (RB // 4))
            total = None
            for j in range(WIDTH // HD):
                cols = slice(j * HD, (j + 1) * HD)
                part = tok[c, rows, cols].astype(F32)
                square = part * part
                total = square if total is None else total + square
                tok[c, rows, cols] = (part * gain[cols].astype(F32)[None, :]).astype(BF16)
            acc.append(total)
        total = jnp.concatenate(acc, axis=0)
        s1[c] = project(0, c)
        s1_copy(c).start()
        s2[0, c] = project(1, c)
        s2_copy(0, c).start()
        s2[1, c] = project(2, c)
        s2_copy(1, c).start()
        row = lax.dot_general(
            jnp.ones((8, HD), F32), total, NT, precision=lax.Precision.HIGHEST, preferred_element_type=F32
        )
        ssq[h, c] = row[0:1, :]
        return carry

    lax.fori_loop(0, NC, first, 0)

    def ssq_copy(k):
        return remote(ssq.at[h], ssq.at[h], ssq_ss.at[k], ssq_rs.at[k], (r, mod(h + k + 1, 8)))

    for k in range(7):
        ssq_copy(k).start()

    def by_request(n, carry):
        mine = owner[n]

        def look(m, found):
            before = (m < n).astype(jnp.int32)
            return found[0] + (owner[m] == mine).astype(jnp.int32) * before, found[1] + lens[m] * before

        rank, begin = lax.fori_loop(0, NPD, look, (jnp.int32(0), jnp.int32(0)))
        req_slot[n] = mine * CAP + rank
        req_start[n] = begin
        return carry

    def by_rows(natural, rows):
        for t in range(STEPS):
            for g in range(GROUP):
                rows[:, t * GROUP + g, :] = natural[t, :, g * HD:(g + 1) * HD].astype(rows.dtype)

    def queries_by_slot():
        lax.fori_loop(0, NPD, by_request, 0)
        request = lax.broadcasted_iota(jnp.int32, (OWNERS * CAP, NPD), 1)
        held = jnp.full((OWNERS * CAP, NPD), -1, jnp.int32)
        for n in range(NPD):
            held = jnp.where(request == n, req_slot[n], held)
        slot = lax.broadcasted_iota(jnp.int32, (OWNERS * CAP, NPD), 0)
        chosen = jnp.where(held == slot, 1.0, 0.0).astype(BF16)
        for t in range(STEPS):
            for g in range(GROUP):
                part = jnp.dot(chosen, arr_query[t, :, g * HD:(g + 1) * HD], preferred_element_type=F32)
                slot_query[:, t * GROUP + g, :] = part

    def steps_by_rows(natural, rows):
        rows[...] = jnp.zeros(rows.shape, rows.dtype)
        for t in range(STEPS):
            for half in range(2):
                rows[half, :, t, :] = natural[t, :, half * HD:(half + 1) * HD].astype(rows.dtype)

    by_rows(res_query, rq)
    steps_by_rows(res_step, rstep)
    by_rows(arr_query, aq)
    steps_by_rows(arr_step, astep)

    def add(*parts):
        return functools.reduce(jnp.add, [part.astype(F32) for part in parts])

    def straight(c, carry):
        pd[0, c] = project(5, c)
        pd[1, c] = project(6, c)
        x_copy(1 - mod(c, 2), c).start()
        return carry

    def second(c, carry):
        p20[c] = project(3, c)
        p01[c] = project(4, c)
        p00[c] = project(7, c)
        return carry

    def to_far(c):
        s1_copy(c).wait_recv()
        p20[c] = add(p20[c], s1r[c]).astype(BF16)
        r2_copy(c).start()

    def to_near(c):
        d = mod(c, 2)
        r2_copy(c).wait_recv()
        pd[d, c] = add(pd[d, c], r2r[c]).astype(BF16)
        x_copy(d, c).start()

    def to_z(c, carry):
        s2_copy(0, c).wait_recv()
        s2_copy(1, c).wait_recv()
        p01[c] = add(p01[c], s2r[0, c], s2r[1, c]).astype(BF16)
        z2_copy(c).start()
        return carry

    col = lax.broadcasted_iota(jnp.int32, (ROWS, CACHE + STEP_PAD), 1)
    row_step = lax.broadcasted_iota(jnp.int32, (ROWS, CACHE + STEP_PAD), 0) // GROUP
    recent_valid = (col >= CACHE) & (col - CACHE <= row_step)

    def residents(i, carry):
        group = [i * 4 + k for k in range(4)]
        keys, values = [
            [
                jnp.concatenate([cach[i, k, :, half * HD:(half + 1) * HD], rstep[half, n].astype(BF16)], axis=0)
                for k, n in enumerate(group)
            ]
            for half in range(2)
        ]
        scores = []
        for k, n in enumerate(group):
            part = lax.dot_general(rq[n].astype(BF16), keys[k], NT, preferred_element_type=F32)
            scores.append(jnp.where((col < cache_lens[n]) | recent_valid, part, -1e30))
        scores = jnp.concatenate(scores, axis=0)
        highest = jnp.max(scores, axis=1, keepdims=True)
        raised = jnp.exp2((scores - highest) * SCALE)
        total = jnp.sum(raised, axis=1, keepdims=True)
        raised = raised.astype(BF16)
        for k, n in enumerate(group):
            rows = slice(k * ROWS, (k + 1) * ROWS)
            result = jnp.dot(raised[rows], values[k], preferred_element_type=F32)
            done_res[n] = result / total[rows]
        return carry

    def shared(zx, name, cx):
        rows = held[zx, name, cx]
        dy = where[name] if cx == 0 else mod(4 - where[name], 4)
        slots = pl.ds(pl.multiple_of(req_at(zx, dy, cx) * CAP, CAP), CAP)
        queries = slot_query[slots].reshape(CAP * ROWS, HD).astype(BF16)
        scores = lax.dot_general(queries, rows[:, :HD], NT, preferred_element_type=F32)
        highest = jnp.max(scores, axis=1, keepdims=True)
        raised = jnp.exp2((scores - highest) * SCALE)
        total = jnp.sum(raised, axis=1, keepdims=True)
        result = jnp.dot(raised.astype(BF16), rows[:, HD:], preferred_element_type=F32) / total
        level = jnp.broadcast_to(highest * SCALE + jnp.log2(total), (CAP * ROWS, HD))
        pacc[slots] = result.astype(BF16).reshape(CAP, ROWS, HD)
        plse[slots] = level.reshape(CAP, ROWS, HD)

    def shared_pair(zx, name):
        shared(zx, name, 0)
        wait_prefix((zx, name, 1))
        shared(zx, name, 1)

    def middle(c, carry):
        to_far(c)
        to_near(c - 1)
        return residents(c, carry)

    w_copy(5).wait()
    w_copy(6).wait()
    lax.fori_loop(0, NC, straight, 0)
    w_copy(3).wait()
    w_copy(4).wait()
    w_copy(7).wait()
    lax.fori_loop(0, NC, second, 0)
    queries_by_slot()
    for g in range(8):
        cache_copy(g).wait()
    to_far(0)
    residents(0, 0)
    near_prefix(0)
    lax.fori_loop(1, 2, middle, 0)
    shared_pair(0, "own")
    lax.fori_loop(2, 3, middle, 0)
    partner_prefix()
    lax.fori_loop(0, 2, to_z, 0)
    shared_pair(0, "back")
    lax.fori_loop(3, 4, middle, 0)
    shared_pair(0, "front")
    lax.fori_loop(4, 5, middle, 0)
    lax.fori_loop(2, 4, to_z, 0)
    far_prefix(0)
    lax.fori_loop(5, NC, middle, 0)
    lax.fori_loop(4, NC, to_z, 0)
    to_near(NC - 1)
    shared_pair(0, "far")
    near_prefix(1)
    shared_pair(1, "own")
    lax.fori_loop(NC, NPD // 4, residents, 0)
    by_step(done_res, out_res)
    shared_pair(1, "back")
    far_prefix(1)
    shared_pair(1, "front")
    shared_pair(1, "far")

    for k in range(7):
        ssq_copy(k).wait_recv()

    for i in range(TOK // 16, (TOK + WINDOW) // 16):
        kv[i] = jnp.zeros((16, PAIR), BF16)

    def finish(c, carry):
        z2_copy(c).wait_recv()
        x_copy(0, c).wait_recv()
        x_copy(1, c).wait_recv()
        squares = lax.dot_general(
            ssq[:, c, 0, :], jnp.ones((8, HD), F32), TN,
            precision=lax.Precision.HIGHEST, preferred_element_type=F32,
        )
        inverse = lax.rsqrt(squares * (1.0 / D) + EPS)
        total = add(p00[c], z2r[c], xr[0, c], xr[1, c])
        both = jnp.concatenate([total[:, :HD] * inverse, total[:, HD:] * inverse], axis=1)
        kv[pl.ds(pl.multiple_of(c * (RB // 16), RB // 16), RB // 16)] = both.astype(BF16).reshape(RB // 16, 16, PAIR)
        return carry

    lax.fori_loop(0, NC, finish, 0)

    def drain(c, carry):
        s1_copy(c).wait_send()
        s2_copy(0, c).wait_send()
        s2_copy(1, c).wait_send()
        r2_copy(c).wait_send()
        z2_copy(c).wait_send()
        x_copy(0, c).wait_send()
        x_copy(1, c).wait_send()
        return carry

    lax.fori_loop(0, NC, drain, 0)
    for k in range(7):
        ssq_copy(k).wait_send()
    for cp in sends:
        cp.wait_send()


def by_step(rows, natural):
    for t in range(STEPS):
        for g in range(GROUP):
            natural[t, :, g * HD:(g + 1) * HD] = rows[:, t * GROUP + g, :]


def prompts(res, kv, pacc, plse, aq, astep, req_slot, req_start, lens, out_arr, out_res, done_arr):
    out_res[...] = res[...]
    width = WINDOW + STEP_PAD
    key_col = lax.broadcasted_iota(jnp.int32, (ROWS, width), 1)
    key_step = lax.broadcasted_iota(jnp.int32, (ROWS, width), 0) // GROUP
    steps_valid = (key_col >= WINDOW) & (key_col - WINDOW <= key_step)

    def arrivals(i, carry):
        group = [i * 4 + k for k in range(4)]
        scores, values = [], []
        for n in group:
            start, length = req_start[n], lens[n]
            base = lax.shift_right_logical(start, 4)
            offset = lax.bitwise_and(start, 15)
            window = [kv[base + k] for k in range(WINDOW // 16)]
            keys = jnp.concatenate([piece[:, :HD] for piece in window] + [astep[0, n].astype(BF16)], axis=0)
            values.append(jnp.concatenate([piece[:, HD:] for piece in window] + [astep[1, n].astype(BF16)], axis=0))
            part = lax.dot_general(aq[n].astype(BF16), keys, NT, preferred_element_type=F32)
            valid = ((key_col >= offset) & (key_col < offset + length)) | steps_valid
            scores.append(jnp.where(valid, part, -1e30))
        slots = [req_slot[n] for n in group]
        scores = jnp.concatenate(scores, axis=0) * SCALE
        level = jnp.concatenate([plse[slot] for slot in slots], axis=0)
        highest = jnp.maximum(jnp.max(scores, axis=1, keepdims=True), level)
        raised = jnp.exp2(scores - highest[:, :width])
        before = jnp.exp2(level - highest)
        total = jnp.sum(raised, axis=1, keepdims=True) + before
        inverse = 1.0 / total
        raised = raised.astype(BF16)
        for k, n in enumerate(group):
            rows = slice(k * ROWS, (k + 1) * ROWS)
            result = jnp.dot(raised[rows], values[k], preferred_element_type=F32)
            done_arr[n] = (result + pacc[slots[k]] * before[rows]) * inverse[rows]
        return carry

    lax.fori_loop(0, NPD // 4, arrivals, 0)
    by_step(done_arr, out_arr)


def fused(*operands):
    vmem = pl.BlockSpec(memory_space=pltpu.VMEM)
    smem = pl.BlockSpec(memory_space=pltpu.SMEM)
    hbm = pl.BlockSpec(memory_space=pl.ANY)
    dma = pltpu.SemaphoreType.DMA
    block = pltpu.VMEM((NC, RB, PAIR), BF16)
    pair = pltpu.VMEM((2, NC, RB, PAIR), BF16)
    by_rows = pltpu.VMEM((NPD, ROWS, HD), F32)
    steps = pltpu.VMEM((2, NPD, STEP_PAD, HD), F32)
    scratch = [
        by_rows, steps, by_rows,
        pltpu.VMEM((NC, RB, WIDTH), BF16),
        pltpu.VMEM((8, WIDTH, PAIR), BF16),
        pltpu.VMEM((8, NPD // 8, CACHE, PAIR), BF16),
        [pltpu.VMEM((PREFIX, PAIR), BF16)] * (OWNERS - 1),
        block, pair, block, block, pair, block,
        block, pair, block, block, pair,
        pltpu.VMEM((8, NC, 1, RB), F32),
        pltpu.VMEM((OWNERS * CAP, ROWS, HD), F32),
        dma((NC,)), dma((8,)), dma((8,)),
        dma((NC,)), dma((NC,)), dma((2, NC)), dma((2, NC)), dma((NC,)), dma((NC,)),
        dma((NC,)), dma((NC,)), dma((2, NC)), dma((2, NC)),
        dma((7,)), dma((7,)), dma((15,)), dma((15,)),
    ]
    out = jax.ShapeDtypeStruct((STEPS, NPD, WIDTH), F32)
    slots = (OWNERS * CAP, ROWS, HD)
    numbers = jax.ShapeDtypeStruct((NPD,), jnp.int32)
    res, *rest = pl.pallas_call(
        kernel,
        out_shape=(
            out,
            jax.ShapeDtypeStruct(((TOK + WINDOW) // 16, 16, PAIR), BF16),
            jax.ShapeDtypeStruct(slots, BF16),
            jax.ShapeDtypeStruct(slots, F32),
            jax.ShapeDtypeStruct((NPD, ROWS, HD), BF16),
            jax.ShapeDtypeStruct((2, NPD, STEP_PAD, HD), BF16),
            numbers,
            numbers,
        ),
        in_specs=[hbm, vmem, hbm, smem, smem, vmem, vmem, vmem, vmem, hbm, vmem, smem],
        out_specs=(vmem,) * 6 + (smem,) * 2,
        scratch_shapes=scratch,
        compiler_params=pltpu.CompilerParams(
            collective_id=0, has_side_effects=True, vmem_limit_bytes=63 * 2**20
        ),
        cost_estimate=pl.CostEstimate(flops=18 * 10**9, bytes_accessed=30 * 10**6, transcendentals=6 * 10**6),
        name="prefill_decode",
    )(*operands)
    return pl.pallas_call(
        prompts,
        out_shape=(out, out),
        in_specs=[vmem] * 6 + [smem] * 3,
        out_specs=(vmem, vmem),
        scratch_shapes=[by_rows],
        compiler_params=pltpu.CompilerParams(vmem_limit_bytes=63 * 2**20),
        cost_estimate=pl.CostEstimate(flops=10**8, bytes_accessed=7 * 10**6, transcendentals=3 * 10**5),
        name="prompts",
    )(res, *rest, operands[3])


def shards(
    tokens, norm_gain, kv_weight, prompt_lens, owner_of, arr_query, arr_step_kv, prefix_kv,
    res_query, res_cache, res_step_kv, cache_lens,
):
    return fused(
        tokens.reshape(NC, RB, WIDTH), norm_gain, kv_weight, prompt_lens.reshape(NPD), owner_of.reshape(NPD), arr_query, arr_step_kv,
        prefix_kv, res_query, res_cache.reshape(8, NPD // 8, CACHE, PAIR), res_step_kv, cache_lens,
    )


def solution(mesh):
    in_specs = (
        P("req", "head"),
        P("head"),
        P("head", None),
        P("req", None),
        P("req", None),
        P(None, "req", "head"),
        P(None, "req", "head"),
        P("req", "head"),
        P(None, "req", "head"),
        P("req", None, "head"),
        P(None, "req", "head"),
        P("req"),
    )
    out_specs = (P(None, "req", "head"), P(None, "req", "head"))
    return jax.shard_map(shards, mesh=mesh, in_specs=in_specs, out_specs=out_specs, check_vma=False)
```
